128 devices in a mesh: grp: 2 (over core), dom: 64 (over y, z, x).
Axes of the slice: x: 4, y: 4, z: 4, core: 2. Of those that a mesh axis runs over, the one named last changes fastest.
Arguments:
- velocity: float32 [4096, 32, 256], P(('grp', 'dom')), may hold values from -6 to 6
- forcing: float32 [4096, 32, 256], P(('grp', 'dom')), may hold values from -3 to 3
- mass: float32 [4096, 32, 256], P(('grp', 'dom')), may hold values from 0.05 to 10
- sample_index: int32 [262144], P(('grp', 'dom')), may hold values from 0 to 262143
- partition: int32 [262144], P(('grp', 'dom')), may hold values from 0 to 262143, each once
- edge_source: int32 [1048576], P(('grp', 'dom')), may hold values from 0 to 2047
- edge_target: int32 [1048576], P(('grp', 'dom')), may hold values from 0 to 2047
- edge_valid: int32 [1048576], P(('grp', 'dom')), may hold values 0 or 1
- w_in: float32 [128], replicated, may hold values from -4 to 4
- b_in: float32 [128], replicated, may hold values from -3 to 3
- layer_weights: float32 [2, 256, 128], replicated, may hold values from -0.375 to 0.375
- layer_bias: float32 [2, 128], replicated, may hold values from -2 to 2
- w_out: float32 [128], replicated, may hold values from -0.5 to 0.5
Outputs:
- new_velocity: float32 [4096, 32, 256], P(('grp', 'dom'))
- loss: float32 [], replicated
- grad_w_in: float32 [128], replicated
- grad_b_in: float32 [128], replicated
- grad_layer_weights: float32 [2, 256, 128], replicated
- grad_layer_bias: float32 [2, 128], replicated
- grad_w_out: float32 [128], replicated
The draws below stay inside these ranges and needn't reach their ends.
Inputs may be any that keep to these rules, and one draw needn't show every extreme that they name: partition names every sampled node exactly once.
All inputs are finite; a program needn't handle non-finite values. No bound on the sum of `edge_valid` on one device may be relied on, other than what follows from the above.
Results may differ from the reference program's by a relative error of at most 0.0006.
Values sent between devices are 32-bit elements; how exact they have to be, the bound alone decides.
A program may use at most 128 MiB of HBM per device.

```python
import math
import jax
import jax.numpy as jnp
from jax import lax

NP = 8
ELX = 4
STEPS = 2
ITERS = 6
WIDTH = 128
LAYERS = 2
SAMPLES = 2048
NX = 4096
NY = 32
NZ = 256
NODES_DEV = 262144
TRAIN_NODES = 262144
EDGES_DEV = 8192
EDGES = 1048576
N_GRP = 2
N_DOM = 64


def draw_mass(key, part):
    key = jax.random.fold_in(key, 11)
    key_flip = jax.random.fold_in(key, 1)
    key_level = jax.random.fold_in(key, 2)
    key_node = jax.random.fold_in(key, 3)
    blocks = NX // (NP * ELX)
    flipped = jax.random.randint(key_flip, (), 0, 2)
    parity = (jnp.arange(blocks, dtype=jnp.int32) + flipped) % 2
    heavy_block = parity == 1
    spread = jax.random.uniform(key_level, (blocks,), jnp.float32, 0.0, math.log(2.0))
    levels = jnp.where(heavy_block, 4.0 * jnp.exp(spread), 0.1 * jnp.exp(spread)).astype(jnp.float32)
    factor = jnp.exp(jax.random.uniform(key_node, (NX, NY, NZ), jnp.float32, math.log(0.5), math.log(1.25)))
    plane_level = jnp.repeat(levels, NP * ELX)
    return (plane_level[:, None, None] * factor).astype(jnp.float32)


def with_ends(result, own_key, least, high):
    shape = result.shape
    index_at = [jax.random.randint(jax.random.fold_in(own_key, axis), (), 0, shape[axis]) for axis in range(len(shape))]
    result = result.at[tuple(index_at)].set(least)
    longest = shape.index(max(shape))
    index_at[longest] = (index_at[longest] + 1) % shape[longest]
    return result.at[tuple(index_at)].set(high)


def block_levels(key, shape, split, least, top_value):
    loudness = 1.0
    for axis_at, parts in split:
        steps = jax.random.uniform(jax.random.fold_in(jax.random.fold_in(key, 6), axis_at), (parts,), jnp.float32, least / len(split), top_value / len(split))
        loudness = loudness * jnp.repeat(jnp.exp(steps), shape[axis_at] // parts).reshape((-1,) + (1,) * (len(shape) - 1 - axis_at))
    return loudness


def normal_values(own_key, shape, scale, limit, pieces=(), kind=jnp.bfloat16):
    drawn = jax.random.normal(own_key, shape, jnp.float32) * scale
    if len(pieces) > 0:
        drawn = block_levels(own_key, shape, pieces, -0.22, 0.18) * drawn
    return jnp.clip(drawn, min=-limit, max=limit).astype(kind)


def setup_inputs(seed: int = 0) -> dict:
    key_list = jax.random.split(jax.random.key(seed), 14)
    velocity = normal_values(key_list[0], (NX, NY, NZ), 1.0, 6.0, ((0, 128),), jnp.float32)
    forcing = normal_values(key_list[1], (NX, NY, NZ), 0.5, 3.0, ((0, 128),), jnp.float32)
    mass = draw_mass(jax.random.fold_in(key_list[13], 71), 0)
    sample_index = with_ends(jax.random.randint(key_list[3], (TRAIN_NODES,), 0, NODES_DEV), jax.random.fold_in(key_list[3], 1), 0, NODES_DEV - 1).astype(jnp.int32)
    partition = jax.random.permutation(key_list[4], TRAIN_NODES).astype(jnp.int32)
    edge_source = with_ends(jax.random.randint(key_list[5], (EDGES,), 0, SAMPLES), jax.random.fold_in(key_list[5], 1), 0, SAMPLES - 1).astype(jnp.int32)
    edge_target = with_ends(jax.random.randint(key_list[6], (EDGES,), 0, SAMPLES), jax.random.fold_in(key_list[6], 1), 0, SAMPLES - 1).astype(jnp.int32)
    edge_valid = with_ends((jax.random.randint(key_list[7], (EDGES,), 0, 4) < 3).astype(jnp.int32), jax.random.fold_in(key_list[7], 1), 0, 1)
    w_in = normal_values(key_list[8], (WIDTH,), 1.0, 4.0, (), jnp.float32)
    b_in = normal_values(key_list[9], (WIDTH,), 0.5, 3.0, (), jnp.float32)
    layer_weights = normal_values(key_list[10], (LAYERS, 2 * WIDTH, WIDTH), (2 * WIDTH) ** -0.5, 0.375, (), jnp.float32)
    layer_bias = normal_values(key_list[11], (LAYERS, WIDTH), 0.3, 2.0, (), jnp.float32)
    w_out = normal_values(key_list[12], (WIDTH,), WIDTH ** -0.5, 0.5, (), jnp.float32)
    return dict(velocity=velocity, forcing=forcing, mass=mass, sample_index=sample_index, partition=partition, edge_source=edge_source, edge_target=edge_target, edge_valid=edge_valid, w_in=w_in, b_in=b_in, layer_weights=layer_weights, layer_bias=layer_bias, w_out=w_out)


penalty = 2.0
agg_scale = 0.25

def element_stiffness():
    rows = jnp.arange(8, dtype=jnp.int32)[:, None]
    cols = jnp.arange(8, dtype=jnp.int32)[None, :]
    spread = jnp.abs(rows - cols).astype(jnp.float32)
    return 2.5 * (rows == cols).astype(jnp.float32) - jnp.exp(-spread)

def along(field, stiff, axis):
    moved = jnp.moveaxis(field, axis, 0)
    length = moved.shape[0]
    blocks = moved.reshape((length // 8, 8) + moved.shape[1:])
    mixed = jnp.einsum('ij,ejyz->eiyz', stiff, blocks, precision=lax.Precision.HIGHEST)
    return jnp.moveaxis(mixed.reshape(moved.shape), 0, axis)

def face_jumps(field, axis, wrap):
    length = field.shape[axis]
    shape = [1, 1, 1]
    shape[axis] = length
    place = jnp.arange(length, dtype=jnp.int32).reshape(shape)
    following = jnp.roll(field, -1, axis)
    preceding = jnp.roll(field, 1, axis)
    last = place % 8 == 7
    first = place % 8 == 0
    if not wrap:
        last = last & (place < length - 1)
        first = first & (place > 0)
    return jnp.where(last, field - following, 0.0) + jnp.where(first, field - preceding, 0.0)

def operate(field, mass):
    stiff = element_stiffness()
    total = along(field, stiff, 0) + along(field, stiff, 1) + along(field, stiff, 2)
    jumps = face_jumps(field, 0, True) + face_jumps(field, 1, False) + face_jumps(field, 2, True)
    return mass * field + total + penalty * jumps

def encode(w_in, b_in, feats):
    return jnp.tanh(feats[:, None] * w_in[None, :] + b_in[None, :])

def propagate(weight, bias, state, source, target_node, valid):
    carried = state[source] * valid[:, None].astype(jnp.float32)
    summed = jax.ops.segment_sum(carried, target_node, num_segments=state.shape[0]) * agg_scale
    joined = jnp.concatenate([state, summed], axis=1)
    return state + jnp.tanh(jnp.dot(joined, weight, precision=lax.Precision.HIGHEST) + bias[None, :])

def readout(w_out, state, target, total):
    pred = jnp.dot(state, w_out, precision=lax.Precision.HIGHEST)
    return jnp.sum((pred - target) ** 2) / total

def block_loss(params, feats, target, source, target_node, valid):
    w_in, b_in, layer_weights, layer_bias, w_out = params
    state = encode(w_in, b_in, feats)
    for layer in range(LAYERS):
        state = propagate(layer_weights[layer], layer_bias[layer], state, source, target_node, valid)
    return readout(w_out, state, target, jnp.float32(TRAIN_NODES))

def reference(velocity, forcing, mass, sample_index, partition, edge_source, edge_target, edge_valid, w_in, b_in, layer_weights, layer_bias, w_out):
    devices = N_GRP * N_DOM
    field = velocity
    picks = sample_index.reshape(devices, SAMPLES)
    snapshots = []
    for step in range(STEPS):
        rhs = mass * field + forcing
        guess = field
        residual = rhs - operate(guess, mass)
        direction = residual
        norm_now = jnp.sum(residual * residual)
        for it in range(ITERS):
            image = operate(direction, mass)
            alpha = norm_now / jnp.sum(direction * image)
            guess = guess + alpha * direction
            residual = residual - alpha * image
            norm_next = jnp.sum(residual * residual)
            direction = residual + norm_next / norm_now * direction
            norm_now = norm_next
        field = guess
        flat = field.reshape(devices, -1)
        snapshots.append(jnp.take_along_axis(flat, picks, axis=1).reshape(-1))
    feats = snapshots[0][partition].reshape(devices, SAMPLES)
    target = snapshots[STEPS - 1][partition].reshape(devices, SAMPLES)
    params = (w_in, b_in, layer_weights, layer_bias, w_out)
    blocks = (feats, target, edge_source.reshape(devices, EDGES_DEV), edge_target.reshape(devices, EDGES_DEV), edge_valid.reshape(devices, EDGES_DEV))

    def one_block(block):
        return jax.value_and_grad(block_loss)(params, *block)
    losses, grads = lax.map(one_block, blocks)
    grads = jax.tree.map(lambda g: lax.optimization_barrier(jnp.sum(g, axis=0)), grads)
    return (field, jnp.sum(losses), grads[0], grads[1], grads[2], grads[3], grads[4])
```

```python
import functools

import jax
import jax.numpy as jnp
import ml_dtypes
import numpy as np
from jax import lax
from jax.experimental import pallas as pl
from jax.experimental.pallas import tpu as pltpu
from jax.sharding import PartitionSpec as P

MESH = pl.DeviceIdType.MESH
F32 = jnp.float32
BF16 = jnp.bfloat16

STEPS = 2
LAYERS = 2
PENALTY = 2.0
AGG_SCALE = 0.25
NODES = 2048
EDGES = 8192
ROWS = 1024
PLANE = 32
GROUPS, DOMS, LINE, SHEET = 2, 64, 4, 16

CENTER = 14.125
HALF = 12.575
GAIN = 2.0 / HALF
PIVOT = 1e-6
REACH = GAIN * GAIN * float(sum(np.exp(-2.0 * i) for i in range(1, 8)))
CHIP_ORDER = [0] + sorted(
    range(1, DOMS), key=lambda o: -sum(min(c, 4 - c) for c in (o % 4, o // 4 % 4, o // 16))
)
FAR_ORDER = [0] + sorted(range(1, 16), key=lambda o: -(min(o % 4, 4 - o % 4) + min(o // 4, 4 - o // 4)))


def split_np(matrix):
    high = matrix.astype(np.float32).astype(ml_dtypes.bfloat16)
    low = (matrix - high.astype(np.float64)).astype(np.float32).astype(ml_dtypes.bfloat16)
    return high, low


def element_matrix():
    at = np.arange(8)
    return 2.5 * np.eye(8) - np.exp(-np.abs(at[:, None] - at[None, :]).astype(np.float64))


def line_matrix(length, wrap):
    matrix = np.kron(np.eye(length // 8), element_matrix())
    for last in range(7, length, 8):
        follow = (last + 1) % length
        if follow == 0 and not wrap:
            continue
        matrix[last, last] += PENALTY
        matrix[follow, follow] += PENALTY
        matrix[last, follow] -= PENALTY
        matrix[follow, last] -= PENALTY
    return matrix


def field_matrices():
    ends = np.zeros(8)
    ends[0] = ends[7] = PENALTY
    sheet = np.kron(element_matrix() + np.diag(ends), np.eye(32)) + np.kron(np.eye(8), line_matrix(32, False))
    sheet_high, sheet_low = split_np(GAIN * sheet)
    span_high, span_low = split_np(GAIN * line_matrix(256, True))
    left = np.concatenate([sheet_high, sheet_low, sheet_high], axis=1)
    right = np.concatenate([span_high, span_low, span_high], axis=0)
    edge = np.concatenate([sheet_high[:32, :32], sheet_low[:32, :32], sheet_high[:32, :32]], axis=1)
    return left, right, edge


def split(value):
    high = value.astype(BF16)
    return high, (value - high.astype(F32)).astype(BF16)


def mm(left, right):
    return jnp.dot(left, right, preferred_element_type=F32)


def mm_lanes(left, right):
    return lax.dot_general(left, right, (((1,), (1,)), ((), ())), preferred_element_type=F32)


def wide(tile):
    two = jnp.concatenate([tile, tile], axis=1)
    return jnp.concatenate([two, two], axis=0)


def fold(value):
    half = value[:8] + value[8:]
    return half[:, :128] + half[:, 128:]


def solve(matrix, rhs):
    n = len(rhs)
    rows = [list(row) for row in matrix]
    right = list(rhs)
    lower = {}
    inverse = []
    for k in range(n):
        pivot = rows[k][k]
        inverse.append(jnp.where(pivot > PIVOT * matrix[k][k], 1.0 / pivot, 0.0))
        for i in range(k + 1, n):
            factor = rows[k][i] * inverse[k]
            lower[i, k] = factor
            for j in range(i, n):
                rows[i][j] = rows[i][j] - factor * rows[k][j]
            right[i] = right[i] - factor * right[k]
    out = [None] * n
    for k in reversed(range(n)):
        value = right[k] * inverse[k]
        for i in range(k + 1, n):
            value = value - lower[i, k] * out[i]
        out[k] = value
    return out


def image_rows(gram, count):
    out = []
    for i in range(count):
        out.append(
            [CENTER * a + (0.5 * HALF) * (b + c) for a, b, c in zip(gram[i], gram[i + 1], gram[abs(i - 1)])]
        )
    return out


def image_coefs(coefs):
    out = [None] * (len(coefs) + 1)

    def add(at, value):
        out[at] = value if out[at] is None else out[at] + value

    for j, c in enumerate(coefs):
        add(j, CENTER * c)
        if j == 0:
            add(1, HALF * c)
        else:
            add(j + 1, (0.5 * HALF) * c)
            add(j - 1, (0.5 * HALF) * c)
    return out


def index_row(index_ref, i):
    return jnp.concatenate([index_ref[2 * i : 2 * i + 1, :], index_ref[2 * i + 1 : 2 * i + 2, :]], axis=1)


def onehot_rows(index_ref, out_ref):
    for i in range(8):
        row = index_row(index_ref, i) >> 8

        def body(c, carry):
            at = pl.multiple_of(c * 128, 128)
            place = lax.broadcasted_iota(jnp.int32, (128, 256), 0) + at
            out_ref[pl.ds(at, 128), i * 256 : (i + 1) * 256] = jnp.where(place == row, 1.0, 0.0).astype(BF16)
            return carry

        lax.fori_loop(0, ROWS // 128, body, 0)


def pick(table, index_ref, onehot_ref, write):
    both = jnp.concatenate(split(table.T), axis=0)
    place = lax.broadcasted_iota(jnp.int32, (256, 256), 0)
    for i in range(8):
        rows = mm(both, onehot_ref[:, i * 256 : (i + 1) * 256])
        rows = rows[:256] + rows[256:]
        column = index_row(index_ref, i) & 255
        write(i, jnp.sum(jnp.where(place == column, rows, 0.0), axis=0, keepdims=True))


def shifted(coefs):
    out = [None] * (len(coefs) + 1)

    def add(at, value):
        out[at] = value if out[at] is None else out[at] + value

    for i, c in enumerate(coefs):
        if i == 0:
            add(1, c)
        else:
            add(i + 1, 0.5 * c)
            add(i - 1, 0.5 * c)
    return out


def merged(parts):
    out = []
    for factor, coefs in parts:
        for i, c in enumerate(coefs):
            value = c if factor is None else factor * c
            if i < len(out):
                out[i] = out[i] + value
            else:
                out.append(value)
    return out


def core_peer(grp, dom, o):
    hop = CHIP_ORDER[o]
    y, z, x = (dom // 16 + hop // 16) % 4, (dom // 4 + hop // 4) % 4, (dom + hop) % 4
    return grp, y * 16 + z * 4 + x


def steps_kernel(
    vel, force, mass, sample, part, left_mat, right_mat, edge_mat,
    out, feats, target,
    basis, stage, ghost, first, beside, dots, near, far, table, hot_sample, hot_part,
    halo_s, halo_r, first_s, first_r, near_s, near_r, far_s, far_r, peer_s, peer_r, core_s, core_r,
):
    grp = lax.axis_index("grp")
    dom = lax.axis_index("dom")
    me = grp * DOMS + dom
    line = dom % LINE
    sheet = dom // LINE
    near_me = grp * LINE + line

    def near_peer(o):
        other = (near_me + o) % (GROUPS * LINE)
        return other, (other // LINE, sheet * LINE + other % LINE)

    def far_peer(o):
        hop = FAR_ORDER[o]
        other = (sheet // 4 + hop // 4) % 4 * 4 + (sheet + hop) % 4
        return other, (grp, other * LINE + line)

    other_core = (1 - grp, dom)
    after = (me + 1) % (GROUPS * DOMS)
    before = (me + GROUPS * DOMS - 1) % (GROUPS * DOMS)
    after_id = (after // DOMS, after % DOMS)
    before_id = (before // DOMS, before % DOMS)

    barrier = pltpu.get_barrier_semaphore()
    greeted = [core_peer(grp, dom, o) for o in range(1, DOMS)] + [near_peer(o)[1] for o in range(1, 8)]
    greeted += [after_id, before_id]
    for who in greeted:
        pl.semaphore_signal(barrier, inc=1, device_id=who, device_id_type=MESH)
    pl.semaphore_wait(barrier, len(greeted))

    def remote(src, dst, send, recv, who):
        return pltpu.make_async_remote_copy(
            src_ref=src, dst_ref=dst, send_sem=send, recv_sem=recv, device_id=who, device_id_type=MESH
        )

    sides = ((0, 0, 0, before_id), (1, ROWS - PLANE, 7, after_id))
    pull = PENALTY * GAIN

    def products(source, e):
        high, low = split(source[e * 256 : (e + 1) * 256, :])
        rows = mm(left_mat[...], jnp.concatenate([high, high, low], axis=0))
        return rows + mm(jnp.concatenate([high, high, low], axis=1), right_mat[...])

    def store_inner(dest, source, e, value, scale):
        at = e * 256
        top, bottom = value[:PLANE], value[256 - PLANE :]
        if e > 0:
            top = top - scale * source[at - PLANE : at, :]
        if e < 3:
            bottom = bottom - scale * source[at + 256 : at + 256 + PLANE, :]
        dest[at : at + PLANE, :] = top
        dest[at + PLANE : at + 256 - PLANE, :] = value[PLANE : 256 - PLANE]
        dest[at + 256 - PLANE : at + 256, :] = bottom

    def expand(slot, opening, elements):
        src, dst = basis.at[slot], basis.at[slot + 1]
        for e in elements:
            rows = pl.ds(e * 256, 256)
            value = products(src, e) + (GAIN * mass[rows, :] - GAIN * CENTER) * src[rows, :]
            if opening:
                value = 0.5 * value
            else:
                value = value - basis[slot - 1, rows, :]
            store_inner(dst, src, e, value, pull * (0.5 if opening else 1.0))

    def outer(slot, side, plane, scale):
        at = sides[side][1]
        value = basis[slot, at : at + PLANE, :] - scale * plane
        basis[slot, at : at + PLANE, :] = value
        return value

    def along(plane, level, near_rows):
        high, low = split(plane)
        wide_plane = jnp.concatenate([high, high, low], axis=1)
        return near_rows + mm(wide_plane, right_mat[...]) + (GAIN * level - GAIN * CENTER) * plane

    def edge_map(side, plane):
        high, low = split(plane)
        rows = mm(edge_mat[...], jnp.concatenate([high, high, low], axis=0))
        return along(plane, first[side, 1], rows)

    def exchange_copies(ex):
        return [
            remote(stage.at[ex, side], ghost.at[ex, 1 - side], halo_s.at[ex, side], halo_r.at[ex, 1 - side], who)
            for side, _, _, who in sides
        ]

    def exchange_send(ex, slot):
        for side, at, place, _ in sides:
            e = 0 if side == 0 else 3
            high, low = split(basis[slot + 1, e * 256 : (e + 1) * 256, :])
            rows = mm(left_mat[place * PLANE : (place + 1) * PLANE, :], jnp.concatenate([high, high, low], axis=0))
            plane = basis[slot + 1, at : at + PLANE, :]
            own = basis[slot, at : at + PLANE, :]
            stage[ex, side, 0] = own
            stage[ex, side, 1] = plane
            stage[ex, side, 2] = along(plane, mass[at : at + PLANE, :], rows) - own
        for copy in exchange_copies(ex):
            copy.start()

    def exchange_wait(ex, slot, opening):
        for copy in exchange_copies(ex):
            copy.wait()
        scale = pull * (0.5 if opening else 1.0)
        for side, at, _, _ in sides:
            own = basis[slot, at : at + PLANE, :]
            then = outer(slot + 1, side, ghost[ex, side, 0], scale)
            beside[side, 0] = ghost[ex, side, 1] - scale * own
            beside[side, 1] = ghost[ex, side, 2] - scale * edge_map(side, own) - pull * then

    def follow(slot):
        for k in range(2):
            expand(slot + k, False, range(4))
            for side in range(2):
                outer(slot + k + 1, side, beside[side, k], pull)

    def accumulate(pairs, chunks):
        slots = sorted({a for _, a, _ in pairs} | {b for _, _, b in pairs})

        def body(c, carry):
            at = pl.multiple_of(c * 16, 16)
            rows = {s: basis[s, pl.ds(at, 16), :] for s in slots}
            return tuple(acc + fold(rows[a] * rows[b]) for acc, (_, a, b) in zip(carry, pairs))

        carry = tuple(jnp.zeros((8, 128), F32) for _ in pairs)
        carry = lax.fori_loop(0, chunks, body, carry, unroll=4)
        for (i, _, _), acc in zip(pairs, carry):
            dots[i] = acc

    stages = (
        (near, near_s, near_r, near_peer, near_me, GROUPS * LINE),
        (far, far_s, far_r, far_peer, sheet, SHEET),
    )

    def reduce_send(call, which, message):
        buffer, send, recv, peer, mine, n = stages[which]
        buffer[call, mine] = jnp.broadcast_to(message, (8, 128))
        own = buffer.at[call, mine]
        for o in range(1, n):
            remote(own, own, send.at[call, o], recv.at[call, mine], peer(o)[1]).start()

    def reduce_wait(call, which):
        buffer, send, recv, peer, mine, n = stages[which]
        own = buffer.at[call, mine]
        for o in range(1, n):
            other, who = peer(o)
            slot = buffer.at[call, other]
            remote(slot, slot, send.at[call, o], recv.at[call, other], who).wait_recv()
        for o in range(1, n):
            remote(own, own, send.at[call, o], recv.at[call, mine], peer(o)[1]).wait_send()
        total = buffer[call, 0]
        for i in range(1, n):
            total = total + buffer[call, i]
        return total

    def reduce_start(call, count):
        total = jnp.sum(dots[...], axis=1)
        column = jnp.sum(total, axis=1, keepdims=True)
        lane = lax.broadcasted_iota(jnp.int32, (24, 128), 1)
        place = lax.broadcasted_iota(jnp.int32, (24, 128), 0)
        keep = (lane == place) & (place < count)
        reduce_send(call, 0, jnp.sum(jnp.where(keep, column, 0.0), axis=0, keepdims=True))

    def reduce_middle(call):
        reduce_send(call, 1, reduce_wait(call, 0))

    def reduce_end(call, count):
        total = reduce_wait(call, 1)
        return [jnp.broadcast_to(total[:, i : i + 1], (8, 128)) for i in range(count)]

    def peer_copies(snap):
        block = table.at[snap, pl.ds(pl.multiple_of(me * 8, 8), 8)]
        return [remote(block, block, peer_s.at[snap], peer_r.at[snap], core_peer(grp, dom, o)) for o in range(1, DOMS)]

    def wait_peers(snap):
        arrived = table.at[snap, pl.ds(0, 8 * (DOMS - 1))]
        copy = remote(arrived, arrived, peer_s.at[snap], peer_r.at[snap], core_peer(grp, dom, 1))
        copy.wait_recv()
        copy.wait_send()

    def core_block(snap, which):
        return table.at[snap, pl.ds(pl.multiple_of(which * 512, 512), 512)]

    def core_copy(snap):
        block = core_block(snap, grp)
        return remote(block, block, core_s.at[snap], core_r.at[snap], other_core)

    def wait_core(snap):
        block = core_block(snap, 1 - grp)
        remote(block, block, core_s.at[snap], core_r.at[snap], other_core).wait_recv()
        core_copy(snap).wait_send()

    def start_all(copies):
        for copy in copies:
            copy.start()

    def write_to(ref):
        def write(i, row):
            ref[i : i + 1, :] = row

        return write

    def first_copies():
        return [
            remote(ref.at[pl.ds(at, PLANE)], first.at[1 - side, i], first_s.at[side, i], first_r.at[1 - side, i], who)
            for side, at, _, who in sides
            for i, ref in enumerate((vel, mass))
        ]

    start_all(first_copies())
    for e in (0, 3, 1, 2):
        rows = pl.ds(e * 256, 256)
        store_inner(basis.at[0], vel, e, force[rows, :] - (1.0 / GAIN) * products(vel, e), -PENALTY)
    expand(0, True, (0, 3))
    exchange_send(0, 0)
    expand(0, True, (1, 2))
    onehot_rows(sample, hot_sample)
    for copy in first_copies():
        copy.wait()
    for side in range(2):
        outer(0, side, first[side, 0], -PENALTY)
    expand(0, True, (0, 3))
    for copy in exchange_copies(0):
        copy.wait()
    for side, at, _, _ in sides:
        own = basis[0, at : at + PLANE, :]
        given = PENALTY * vel[at : at + PLANE, :]
        mapped = edge_map(side, given)
        then = outer(1, side, ghost[0, side, 0] + given, 0.5 * pull)
        beside[side, 0] = ghost[0, side, 1] + 0.5 * mapped - (0.5 * pull) * own
        beside[side, 1] = (
            ghost[0, side, 2] + 0.5 * edge_map(side, mapped - pull * own) + (0.5 * REACH - 1.0) * given - pull * then
        )

    for step in range(STEPS):
        call = 2 * step
        if step > 0:
            expand(0, True, (0, 3))
            exchange_send(2 * step, 0)
            expand(0, True, (1, 2))
            picked = []
            pick(out[...], sample, hot_sample, lambda i, row: picked.append(row))
            table[step - 1, pl.ds(pl.multiple_of(me * 8, 8), 8), :] = jnp.concatenate(picked, axis=0)
            start_all(peer_copies(step - 1))
            exchange_wait(2 * step, 0, True)
        follow(1)
        index = {}
        for j in range(4):
            for i in range(min(j, 2) + 1):
                index[i, j] = index[j, i] = len(index) - sum(1 for a, b in index if a > b)
        accumulate([(n, i, j) for (i, j), n in index.items() if i <= j], 64)
        reduce_start(call, 9)
        expand(3, False, (0, 3))
        exchange_send(2 * step + 1, 3)
        expand(3, False, (1, 2))
        reduce_middle(call)
        if step == 0:
            onehot_rows(part, hot_part)
        exchange_wait(2 * step + 1, 3, False)
        follow(4)
        m = reduce_end(call, 9)
        gram = [[m[index[i, j]] for j in range(3)] for i in range(4)]
        image = image_rows(gram, 3)
        head = [[image[max(i, j)][min(i, j)] for j in range(3)] for i in range(3)]
        opening = solve(head, gram[0])
        after_three = [-c for c in image_coefs(opening)]
        after_three[0] = 1.0 + after_three[0]
        combos = [after_three, shifted(after_three)]
        for _ in range(2):
            combos.append([2.0 * c for c in shifted(combos[-1])])
            for i, c in enumerate(combos[-3]):
                combos[-1][i] = combos[-1][i] - c
        factors = [[wide(c) for c in coefs] for coefs in combos]
        pairs = [(i, 4 + j) for j in range(3) for i in range(4)]
        pairs += [(4 + i, 4 + j) for j in range(4) for i in range(min(j, 2) + 1)]

        def gather_dots(c, carry):
            at = pl.multiple_of(c * 16, 16)
            rows = [basis[s, pl.ds(at, 16), :] for s in range(7)]
            for coefs in factors:
                value = coefs[0] * rows[0]
                for c_i, row in zip(coefs[1:], rows[1:7]):
                    value = value + c_i * row
                rows.append(value)
            held = rows[:4] + rows[7:]
            return tuple(acc + fold(held[a] * held[b]) for acc, (a, b) in zip(carry, pairs))

        carry = lax.fori_loop(0, 64, gather_dots, tuple(jnp.zeros((8, 128), F32) for _ in pairs))
        for i, acc in enumerate(carry):
            dots[i] = acc
        reduce_start(call + 1, len(pairs))
        if step > 0:
            wait_peers(step - 1)
            core_copy(step - 1).start()
        reduce_middle(call + 1)
        if step > 0:
            wait_core(step - 1)
            pick(table[step - 1], part, hot_part, write_to(feats))
        m = reduce_end(call + 1, len(pairs))
        index = {}
        for n, (a, b) in enumerate(pairs):
            index[a, b] = index[b, a] = n
        cross = image_rows([[m[index[i, 4 + j]] for j in range(3)] for i in range(4)], 3)
        gram = [[m[index[4 + i, 4 + j]] for j in range(3)] for i in range(4)]
        image = image_rows(gram, 3)
        whole = [[None] * 6 for _ in range(6)]
        for i in range(3):
            for j in range(3):
                whole[i][j] = head[i][j]
                whole[3 + i][3 + j] = image[max(i, j)][min(i, j)]
                whole[i][3 + j] = whole[3 + j][i] = cross[i][j]
        coefs = solve(whole, [m[index[i, 4]] for i in range(3)] + gram[0])
        moves = merged([(None, opening), (None, coefs[:3])] + [(coefs[3 + j], combos[j]) for j in range(3)])
        lost = image_coefs(coefs[3:])
        rest = merged([(None, combos[0])] + [(-lost[j], combos[j]) for j in range(4)] + [(-1.0, image_coefs(coefs[:3]))])
        moves = [wide(c) for c in moves]
        rest = [wide(c) for c in rest]
        start = vel if step == 0 else out
        more = step < STEPS - 1

        def advance(c, carry):
            rows = pl.ds(pl.multiple_of(c * 16, 16), 16)
            held = [basis[s, rows, :] for s in range(7 if more else 6)]
            moved = moves[0] * held[0]
            for c_i, row in zip(moves[1:], held[1:]):
                moved = moved + c_i * row
            if more:
                value = mass[rows, :] * moved
                for c_i, row in zip(rest, held):
                    value = value + c_i * row
                basis[0, rows, :] = value
            out[rows, :] = start[rows, :] + moved
            return carry

        lax.fori_loop(0, 64, advance, 0, unroll=2)

    last = STEPS - 1
    picked = []
    pick(out[...], sample, hot_sample, lambda i, row: picked.append(row))
    table[last, pl.ds(pl.multiple_of(me * 8, 8), 8), :] = jnp.concatenate(picked, axis=0)
    start_all(peer_copies(last))
    wait_peers(last)
    core_copy(last).start()
    wait_core(last)
    pick(table[last], part, hot_part, write_to(target))


VMEM = pl.BlockSpec(memory_space=pltpu.VMEM)
SMEM = pl.BlockSpec(memory_space=pltpu.SMEM)
ANY = pl.BlockSpec(memory_space=pl.ANY)


def run_steps(velocity, forcing, mass, sample, part):
    dma = pltpu.SemaphoreType.DMA
    return pl.pallas_call(
        steps_kernel,
        out_shape=(
            jax.ShapeDtypeStruct((ROWS, 256), F32),
            jax.ShapeDtypeStruct((8, 256), F32),
            jax.ShapeDtypeStruct((8, 256), F32),
        ),
        in_specs=[VMEM] * 8,
        out_specs=(VMEM,) * 3,
        scratch_shapes=[
            pltpu.VMEM((7, ROWS, 256), F32),
            pltpu.VMEM((4, 2, 3, PLANE, 256), F32),
            pltpu.VMEM((4, 2, 3, PLANE, 256), F32),
            pltpu.VMEM((2, 2, PLANE, 256), F32),
            pltpu.VMEM((2, 2, PLANE, 256), F32),
            pltpu.VMEM((24, 8, 128), F32),
            pltpu.VMEM((4, 8, 8, 128), F32),
            pltpu.VMEM((4, 16, 8, 128), F32),
            pltpu.VMEM((2, ROWS, 256), F32),
            pltpu.VMEM((ROWS, NODES), BF16),
            pltpu.VMEM((ROWS, NODES), BF16),
            dma((4, 2)), dma((4, 2)),
            dma((2, 2)), dma((2, 2)),
            dma((4, 8)), dma((4, 8)),
            dma((4, 16)), dma((4, 16)),
            dma((2,)), dma((2,)),
            dma((2,)), dma((2,)),
        ],
        compiler_params=pltpu.CompilerParams(
            collective_id=0, has_side_effects=True, vmem_limit_bytes=56 << 20
        ),
        cost_estimate=pl.CostEstimate(flops=30_000_000_000, bytes_accessed=4 << 20, transcendentals=0),
        name="viscous_steps",
    )(velocity, forcing, mass, sample, part, *field_matrices())


def split3(value, axis):
    high, low = split(value)
    return jnp.concatenate([high, high, low], axis=axis)


def split3_other(value, axis):
    high, low = split(value)
    return jnp.concatenate([high, low, high], axis=axis)


HALF_PAGES = 8
COUNT_ROWS = HALF_PAGES * NODES


def count_edges(key_ref, adj, accs):
    def clear(i, carry):
        for acc in accs:
            acc[pl.ds(pl.multiple_of(i * 128, 128), 128), :] = jnp.zeros((128, 128), jnp.int32)
        return carry

    lax.fori_loop(0, COUNT_ROWS // 128, clear, 0)
    place = lax.broadcasted_iota(jnp.int32, (8, 128), 0) * 128 + lax.broadcasted_iota(jnp.int32, (8, 128), 1)
    stream = EDGES // len(accs)

    def add(i, carry):
        for u in range(8):
            keys = [key_ref[c * stream + i * 8 + u] for c in range(len(accs))]
            spots = [pl.ds(pl.multiple_of((k >> 11) * 8, 8), 8) for k in keys]
            held = [acc[spot, :] for acc, spot in zip(accs, spots)]
            for acc, spot, k, value in zip(accs, spots, keys, held):
                word = jnp.full((8, 128), k, jnp.int32)
                one = lax.shift_left(jnp.full((8, 128), 1, jnp.int32), (word >> 6) & 16)
                acc[spot, :] = value + jnp.where((word & 1023) == place, one, 0)
        return carry

    lax.fori_loop(0, stream // 8, add, 0)

    def total(i, carry):
        rows = pl.ds(pl.multiple_of(i * 128, 128), 128)
        value = accs[0][rows, :]
        for acc in accs[1:]:
            value = value + acc[rows, :]
        accs[0][rows, :] = value
        return carry

    lax.fori_loop(0, COUNT_ROWS // 128, total, 0, unroll=2)

    def halves(rows):
        value = accs[0][rows, :]
        return (value & 65535).astype(F32), (value >> 16).astype(F32)

    worst = jnp.zeros((128, 128), F32)
    for page in range(HALF_PAGES):

        def move(i, most):
            at = pl.multiple_of(i * 128, 128)
            for h, value in enumerate(halves(page_rows(at, page, 128))):
                low = value.astype(BF16)
                column = h * 1024 + page * 128
                adj[pl.ds(at, 128), column : column + 128] = low
                most = jnp.maximum(most, jnp.abs(value - low.astype(F32)))
            return most

        worst = lax.fori_loop(0, NODES // 128, move, worst, unroll=2)
    flagged = jnp.max(worst) > 0.0

    @pl.when(flagged)
    def _():
        def keep(i, carry):
            rows = pl.ds(pl.multiple_of(i * 128, 128), 128)
            for acc, value in zip(accs, halves(rows)):
                acc[rows, :] = (value - value.astype(BF16).astype(F32)).astype(jnp.int32)
            return carry

        lax.fori_loop(0, COUNT_ROWS // 128, keep, 0)

    return flagged


def page_rows(start, page, count):
    return pl.ds(start * 8 + page, count, stride=8)


def surrogate_kernel(
    key_ref, feats, target, w_in_ref, b_in_ref, bias_ref, w_out_ref, weights, field,
    out, field_out,
    one, two, three, four, adj, feat_row, target_row, joined, slope, partial, sent, extra, grads, w_fwd, w_bwd, sem,
):
    tiles = NODES // 256
    field_copy = pltpu.make_async_copy(field, field_out, sem)
    field_copy.start()
    accs = (one, two, three, four)
    flagged = count_edges(key_ref, adj, accs)
    for i in range(8):
        feat_row[:, i * 256 : (i + 1) * 256] = feats[i : i + 1, :]
        target_row[:, i * 256 : (i + 1) * 256] = target[i : i + 1, :]
    vectors = [w_in_ref[...], b_in_ref[...], bias_ref[...], w_out_ref[...], jnp.zeros((123, 128), F32)]
    columns = jnp.concatenate(vectors, axis=0).T
    w_in, b_in, w_out = columns[:, 0:1], columns[:, 1:2], columns[:, 4:5]
    biases = (columns[:, 2:3], columns[:, 3:4])
    for layer in range(LAYERS):
        weight = weights[layer]
        w_fwd[layer] = split3_other(weight.T, 1)
        w_bwd[layer] = split3_other(weight, 1)
    grads[...] = jnp.zeros_like(grads)
    extra[...] = jnp.zeros_like(extra)

    def lanes(j):
        return pl.ds(pl.multiple_of(j * 256, 256), 256)

    def send(slot, at, value):
        high, low = split(value)
        sent[slot, 0:128, at] = high
        sent[slot, 128:256, at] = low

    def both(rows):
        return rows[:128] + rows[128:]

    def spill(half, rows):
        return accs[half][rows, :].astype(F32).astype(BF16)

    def gather_extra(slot):
        @pl.when(flagged)
        def _():
            for half in range(2):

                def body(page, carry):
                    rows = both(mm(sent[slot], spill(half, page_rows(0, page, NODES))))
                    extra[:, pl.ds(pl.multiple_of(half * 1024 + page * 128, 128), 128)] = rows
                    return carry

                lax.fori_loop(0, HALF_PAGES, body, 0)

    def scatter_extra(slot):
        @pl.when(flagged)
        def _():
            def body(j, carry):
                rows = jnp.zeros((256, 256), F32)
                for half in range(2):
                    for page in range(HALF_PAGES):
                        column = half * 1024 + page * 128
                        block = spill(half, page_rows(j * 256, page, 256))
                        rows = rows + mm_lanes(sent[slot, :, column : column + 128], block)
                extra[:, lanes(j)] = both(rows)
                return carry

            lax.fori_loop(0, tiles, body, 0)

    def gather(slot, at):
        return AGG_SCALE * (both(mm(sent[slot], adj[:, at])) + extra[:, at])

    def scatter(slot, at):
        return AGG_SCALE * (both(mm_lanes(sent[slot], adj[at, :])) + extra[:, at])

    def opening(j, carry):
        at = lanes(j)
        value = jnp.tanh(w_in * feat_row[:, at] + b_in)
        joined[0, 0:128, at] = value
        send(0, at, value)
        return carry

    lax.fori_loop(0, tiles, opening, 0, unroll=2)

    def update(layer, at):
        joined[layer, 128:256, at] = gather(layer, at)
        bump = jnp.tanh(mm(w_fwd[layer], split3(joined[layer, :, at], 0)) + biases[layer])
        slope[layer, :, at] = 1.0 - bump * bump
        return joined[layer, 0:128, at] + bump

    def back(layer, at, above):
        pre = above * slope[layer, :, at]
        spot = slice(layer * 256, layer * 256 + 256)
        grads[spot, :] = grads[spot, :] + mm_lanes(split3(joined[layer, :, at], 1), split3_other(pre, 1))
        below = mm(w_bwd[layer], split3(pre, 0))
        partial[layer, :, at] = above + below[:128]
        send(2 + layer, at, below[128:])
        return jnp.sum(pre, axis=1, keepdims=True)

    def second(j, carry):
        at = lanes(j)
        value = update(0, at)
        joined[1, 0:128, at] = value
        send(1, at, value)
        return carry

    gather_extra(0)
    lax.fori_loop(0, tiles, second, 0, unroll=8)

    zero = jnp.zeros((128, 1), F32)

    def third(j, carry):
        loss, grad_out, grad_bias = carry
        at = lanes(j)
        value = update(1, at)
        miss = jnp.sum(w_out * value, axis=0, keepdims=True) - target_row[:, at]
        scaled = miss * (2.0 / (NODES * GROUPS * DOMS))
        loss = loss + miss * miss
        grad_out = grad_out + jnp.sum(value * scaled, axis=1, keepdims=True)
        return loss, grad_out, grad_bias + back(1, at, w_out * scaled)

    gather_extra(1)
    loss, grad_out, bias_1 = lax.fori_loop(
        0, tiles, third, (jnp.zeros((1, 256), F32), zero, zero), unroll=8
    )

    def fourth(j, carry):
        at = lanes(j)
        return carry + back(0, at, partial[1, :, at] + scatter(3, at))

    scatter_extra(3)
    bias_0 = lax.fori_loop(0, tiles, fourth, zero, unroll=8)

    def fifth(j, carry):
        grad_in, grad_bias = carry
        at = lanes(j)
        value = joined[0, 0:128, at]
        pre = (partial[0, :, at] + scatter(2, at)) * (1.0 - value * value)
        grad_in = grad_in + jnp.sum(pre * feat_row[:, at], axis=1, keepdims=True)
        return grad_in, grad_bias + jnp.sum(pre, axis=1, keepdims=True)

    scatter_extra(2)
    grad_in, grad_bias = lax.fori_loop(0, tiles, fifth, (zero, zero), unroll=8)
    loss = jnp.sum(loss, axis=1, keepdims=True) * (1.0 / (NODES * GROUPS * DOMS))
    lane = lax.broadcasted_iota(jnp.int32, (128, 128), 1)
    packed = jnp.where(lane == 5, loss, 0.0)
    for i, column in enumerate((grad_in, grad_bias, bias_0, bias_1, grad_out)):
        packed = packed + jnp.where(lane == i, column, 0.0)
    blank = jnp.zeros((3, 128), F32)
    for f in range(128):
        out[f, 0:4, :] = grads[4 * f : 4 * f + 4, :]
        out[f, 4:5, :] = packed[f : f + 1, :]
        out[f, 5:8, :] = blank
    field_copy.wait()


def surrogate(key, feats, target, w_in, b_in, layer_bias, w_out, layer_weights, field):
    return pl.pallas_call(
        surrogate_kernel,
        out_shape=(jax.ShapeDtypeStruct((128, 8, 128), F32), jax.ShapeDtypeStruct((ROWS, 256), F32)),
        in_specs=[SMEM] + [VMEM] * 7 + [ANY],
        out_specs=(VMEM, ANY),
        scratch_shapes=[pltpu.VMEM((COUNT_ROWS + 8, 128), jnp.int32)] * 4
        + [
            pltpu.VMEM((NODES, NODES), BF16),
            pltpu.VMEM((1, NODES), F32),
            pltpu.VMEM((1, NODES), F32),
            pltpu.VMEM((LAYERS, 256, NODES), F32),
            pltpu.VMEM((LAYERS, 128, NODES), F32),
            pltpu.VMEM((LAYERS, 128, NODES), F32),
            pltpu.VMEM((4, 256, NODES), BF16),
            pltpu.VMEM((128, NODES), F32),
            pltpu.VMEM((LAYERS * 256, 128), F32),
            pltpu.VMEM((LAYERS, 128, 768), BF16),
            pltpu.VMEM((LAYERS, 256, 384), BF16),
            pltpu.SemaphoreType.DMA,
        ],
        compiler_params=pltpu.CompilerParams(vmem_limit_bytes=61 << 20),
        name="surrogate",
    )(
        key, feats, target, w_in.reshape(1, 128), b_in.reshape(1, 128), layer_bias, w_out.reshape(1, 128),
        layer_weights, field,
    )


def edge_keys(source, target_node, valid):
    return jnp.where(valid != 0, source * NODES + target_node, NODES * NODES).astype(jnp.int32)


def sum_kernel(
    grads, out, other, total, share, result, core_s, core_r, share_s, share_r, back_s, back_r, last_s, last_r
):
    grp = lax.axis_index("grp")
    dom = lax.axis_index("dom")
    other_core = (1 - grp, dom)
    peers = [core_peer(grp, dom, o) for o in range(1, DOMS)]

    def remote(src, dst, send, recv, who):
        return pltpu.make_async_remote_copy(
            src_ref=src, dst_ref=dst, send_sem=send, recv_sem=recv, device_id=who, device_id_type=MESH
        )

    barrier = pltpu.get_barrier_semaphore()
    for who in peers + [other_core]:
        pl.semaphore_signal(barrier, inc=1, device_id=who, device_id_type=MESH)
    pl.semaphore_wait(barrier, DOMS)

    def half(which):
        return pl.ds(pl.multiple_of(which * DOMS, DOMS), DOMS)

    copy = remote(grads.at[half(1 - grp)], other, core_s, core_r, other_core)
    copy.start()
    copy.wait()
    total[...] = grads[half(grp)] + other[...]
    for _, peer in peers:
        remote(total.at[peer], share.at[dom], share_s, share_r, (grp, peer)).start()
    share[dom] = total[dom]
    arrived = share.at[pl.ds(0, DOMS - 1)]
    copy = remote(arrived, arrived, share_s, share_r, peers[0])
    copy.wait_recv()
    copy.wait_send()
    parts = [share[i] for i in range(DOMS)]
    while len(parts) > 1:
        parts = [a + b for a, b in zip(parts[::2], parts[1::2])]
    mine = grp * DOMS + dom
    result[mine] = parts[0]
    for who in peers:
        remote(result.at[mine], result.at[mine], back_s, back_r, who).start()
    arrived = result.at[pl.ds(0, DOMS - 1)]
    copy = remote(arrived, arrived, back_s, back_r, peers[0])
    copy.wait_recv()
    copy.wait_send()
    own = result.at[half(grp)]
    copy = remote(own, own, last_s, last_r, other_core)
    copy.start()
    out[half(grp)] = result[half(grp)]
    there = result.at[half(1 - grp)]
    remote(there, there, last_s, last_r, other_core).wait_recv()
    out[half(1 - grp)] = result[half(1 - grp)]
    copy.wait_send()


def sum_grads(grads):
    dma = pltpu.SemaphoreType.DMA
    return pl.pallas_call(
        sum_kernel,
        out_shape=jax.ShapeDtypeStruct((128, 8, 128), F32),
        in_specs=[VMEM],
        out_specs=VMEM,
        scratch_shapes=[
            pltpu.VMEM((DOMS, 8, 128), F32),
            pltpu.VMEM((DOMS, 8, 128), F32),
            pltpu.VMEM((DOMS, 8, 128), F32),
            pltpu.VMEM((2 * DOMS, 8, 128), F32),
        ]
        + [dma] * 8,
        compiler_params=pltpu.CompilerParams(collective_id=1, has_side_effects=True, vmem_limit_bytes=32 << 20),
        name="sum_grads",
    )(grads)


def unpack_kernel(tiles, weight_out, in_out, bias_in_out, bias_out, head_out, loss_out):
    for f in range(128):
        weight_out[f // 64, f % 64 * 4 : f % 64 * 4 + 4, :] = tiles[f, 0:4, :]
    rows = tiles[:, 4, :].T
    in_out[...] = rows[0:1, :]
    bias_in_out[...] = rows[1:2, :]
    bias_out[...] = rows[2:4, :]
    head_out[...] = rows[4:5, :]
    loss_out[...] = rows[5:6, 0:1]


def unpack(tiles):
    row = jax.ShapeDtypeStruct((1, 128), F32)
    return pl.pallas_call(
        unpack_kernel,
        out_shape=(
            jax.ShapeDtypeStruct((LAYERS, 256, 128), F32), row, row, jax.ShapeDtypeStruct((2, 128), F32), row,
            jax.ShapeDtypeStruct((1, 1), F32),
        ),
        in_specs=[VMEM],
        out_specs=(VMEM,) * 6,
        name="unpack",
    )(tiles)


def shards(
    velocity, forcing, mass, sample_index, partition, edge_source, edge_target, edge_valid,
    w_in, b_in, layer_weights, layer_bias, w_out,
):
    shape = velocity.shape
    field, feats, target = run_steps(
        velocity.reshape(ROWS, 256), forcing.reshape(ROWS, 256), mass.reshape(ROWS, 256),
        sample_index.reshape(16, 128), partition.reshape(16, 128),
    )
    grads, field = surrogate(
        edge_keys(edge_source, edge_target, edge_valid), feats, target, w_in, b_in, layer_bias, w_out, layer_weights,
        field,
    )
    weight, grad_in, grad_bin, bias, head, loss = unpack(sum_grads(grads))
    return (
        field.reshape(shape), loss.reshape(()), grad_in.reshape(128), grad_bin.reshape(128), weight, bias,
        head.reshape(128),
    )


def solution(mesh):
    many = P(("grp", "dom"))
    block = P(("grp", "dom"), None, None)
    return jax.shard_map(
        shards,
        mesh=mesh,
        in_specs=(block,) * 3 + (many,) * 5 + (P(),) * 5,
        out_specs=(block,) + (P(),) * 6,
        check_vma=False,
    )
```

```python
import functools

import jax
import jax.numpy as jnp
import ml_dtypes
import numpy as np
from jax import lax
from jax.experimental import pallas as pl
from jax.experimental.pallas import tpu as pltpu
from jax.sharding import PartitionSpec as P

MESH = pl.DeviceIdType.MESH
F32 = jnp.float32
BF16 = jnp.bfloat16

STEPS = 2
LAYERS = 2
PENALTY = 2.0
AGG_SCALE = 0.25
NODES = 2048
EDGES = 8192
ROWS = 1024
PLANE = 32
GROUPS, DOMS, LINE, SHEET = 2, 64, 4, 16

CENTER = 14.125
HALF = 12.575
GAIN = 2.0 / HALF
PIVOT = 1e-6
REACH = GAIN * GAIN * float(sum(np.exp(-2.0 * i) for i in range(1, 8)))
CHIP_ORDER = [0] + sorted(
    range(1, DOMS), key=lambda o: -sum(min(c, 4 - c) for c in (o % 4, o // 4 % 4, o // 16))
)
FAR_ORDER = [0] + sorted(range(1, 16), key=lambda o: -(min(o % 4, 4 - o % 4) + min(o // 4, 4 - o // 4)))


def split_np(matrix):
    high = matrix.astype(np.float32).astype(ml_dtypes.bfloat16)
    low = (matrix - high.astype(np.float64)).astype(np.float32).astype(ml_dtypes.bfloat16)
    return high, low


def element_matrix():
    at = np.arange(8)
    return 2.5 * np.eye(8) - np.exp(-np.abs(at[:, None] - at[None, :]).astype(np.float64))


def line_matrix(length, wrap):
    matrix = np.kron(np.eye(length // 8), element_matrix())
    for last in range(7, length, 8):
        follow = (last + 1) % length
        if follow == 0 and not wrap:
            continue
        matrix[last, last] += PENALTY
        matrix[follow, follow] += PENALTY
        matrix[last, follow] -= PENALTY
        matrix[follow, last] -= PENALTY
    return matrix


def field_matrices():
    ends = np.zeros(8)
    ends[0] = ends[7] = PENALTY
    sheet = np.kron(element_matrix() + np.diag(ends), np.eye(32)) + np.kron(np.eye(8), line_matrix(32, False))
    sheet_high, sheet_low = split_np(GAIN * sheet)
    span_high, span_low = split_np(GAIN * line_matrix(256, True))
    left = np.concatenate([sheet_high, sheet_low, sheet_high], axis=1)
    right = np.concatenate([span_high, span_low, span_high], axis=0)
    edge = np.concatenate([sheet_high[:32, :32], sheet_low[:32, :32], sheet_high[:32, :32]], axis=1)
    return left, right, edge


def split(value):
    high = value.astype(BF16)
    return high, (value - high.astype(F32)).astype(BF16)


def mm(left, right):
    return jnp.dot(left, right, preferred_element_type=F32)


def mm_lanes(left, right):
    return lax.dot_general(left, right, (((1,), (1,)), ((), ())), preferred_element_type=F32)


def wide(tile):
    two = jnp.concatenate([tile, tile], axis=1)
    return jnp.concatenate([two, two], axis=0)


def fold(value):
    half = value[:8] + value[8:]
    return half[:, :128] + half[:, 128:]


def solve(matrix, rhs):
    n = len(rhs)
    rows = [list(row) for row in matrix]
    right = list(rhs)
    lower = {}
    inverse = []
    for k in range(n):
        pivot = rows[k][k]
        inverse.append(jnp.where(pivot > PIVOT * matrix[k][k], 1.0 / pivot, 0.0))
        for i in range(k + 1, n):
            factor = rows[k][i] * inverse[k]
            lower[i, k] = factor
            for j in range(i, n):
                rows[i][j] = rows[i][j] - factor * rows[k][j]
            right[i] = right[i] - factor * right[k]
    out = [None] * n
    for k in reversed(range(n)):
        value = right[k] * inverse[k]
        for i in range(k + 1, n):
            value = value - lower[i, k] * out[i]
        out[k] = value
    return out


def image_rows(gram, count):
    out = []
    for i in range(count):
        out.append(
            [CENTER * a + (0.5 * HALF) * (b + c) for a, b, c in zip(gram[i], gram[i + 1], gram[abs(i - 1)])]
        )
    return out


def image_coefs(coefs):
    out = [None] * (len(coefs) + 1)

    def add(at, value):
        out[at] = value if out[at] is None else out[at] + value

    for j, c in enumerate(coefs):
        add(j, CENTER * c)
        if j == 0:
            add(1, HALF * c)
        else:
            add(j + 1, (0.5 * HALF) * c)
            add(j - 1, (0.5 * HALF) * c)
    return out


def index_row(index_ref, i):
    return jnp.concatenate([index_ref[2 * i : 2 * i + 1, :], index_ref[2 * i + 1 : 2 * i + 2, :]], axis=1)


def onehot_rows(index_ref, out_ref):
    for i in range(8):
        row = index_row(index_ref, i) >> 8

        def body(c, carry):
            at = pl.multiple_of(c * 128, 128)
            place = lax.broadcasted_iota(jnp.int32, (128, 256), 0) + at
            out_ref[pl.ds(at, 128), i * 256 : (i + 1) * 256] = jnp.where(place == row, 1.0, 0.0).astype(BF16)
            return carry

        lax.fori_loop(0, ROWS // 128, body, 0)


def pick(table, index_ref, onehot_ref, write):
    both = jnp.concatenate(split(table.T), axis=0)
    place = lax.broadcasted_iota(jnp.int32, (256, 256), 0)
    for i in range(8):
        rows = mm(both, onehot_ref[:, i * 256 : (i + 1) * 256])
        rows = rows[:256] + rows[256:]
        column = index_row(index_ref, i) & 255
        write(i, jnp.sum(jnp.where(place == column, rows, 0.0), axis=0, keepdims=True))


def shifted(coefs):
    out = [None] * (len(coefs) + 1)

    def add(at, value):
        out[at] = value if out[at] is None else out[at] + value

    for i, c in enumerate(coefs):
        if i == 0:
            add(1, c)
        else:
            add(i + 1, 0.5 * c)
            add(i - 1, 0.5 * c)
    return out


def merged(parts):
    out = []
    for factor, coefs in parts:
        for i, c in enumerate(coefs):
            value = c if factor is None else factor * c
            if i < len(out):
                out[i] = out[i] + value
            else:
                out.append(value)
    return out


def core_peer(grp, dom, o):
    hop = CHIP_ORDER[o]
    y, z, x = (dom // 16 + hop // 16) % 4, (dom // 4 + hop // 4) % 4, (dom + hop) % 4
    return grp, y * 16 + z * 4 + x


def steps_kernel(
    vel, force, mass, sample, part, source, target_node, valid, left_mat, right_mat, edge_mat,
    out, feats, target, keys,
    basis, stage, ghost, first, beside, dots, near, far, table, hot_sample, hot_part,
    halo_s, halo_r, first_s, first_r, near_s, near_r, far_s, far_r, peer_s, peer_r, core_s, core_r,
):
    grp = lax.axis_index("grp")
    dom = lax.axis_index("dom")
    me = grp * DOMS + dom
    line = dom % LINE
    sheet = dom // LINE
    near_me = grp * LINE + line

    def near_peer(o):
        other = (near_me + o) % (GROUPS * LINE)
        return other, (other // LINE, sheet * LINE + other % LINE)

    def far_peer(o):
        hop = FAR_ORDER[o]
        other = (sheet // 4 + hop // 4) % 4 * 4 + (sheet + hop) % 4
        return other, (grp, other * LINE + line)

    other_core = (1 - grp, dom)
    after = (me + 1) % (GROUPS * DOMS)
    before = (me + GROUPS * DOMS - 1) % (GROUPS * DOMS)
    after_id = (after // DOMS, after % DOMS)
    before_id = (before // DOMS, before % DOMS)

    barrier = pltpu.get_barrier_semaphore()
    greeted = [core_peer(grp, dom, o) for o in range(1, DOMS)] + [near_peer(o)[1] for o in range(1, 8)]
    greeted += [after_id, before_id]
    for who in greeted:
        pl.semaphore_signal(barrier, inc=1, device_id=who, device_id_type=MESH)

    def remote(src, dst, send, recv, who):
        return pltpu.make_async_remote_copy(
            src_ref=src, dst_ref=dst, send_sem=send, recv_sem=recv, device_id=who, device_id_type=MESH
        )

    sides = ((0, 0, 0, before_id), (1, ROWS - PLANE, 7, after_id))
    pull = PENALTY * GAIN

    def products(source, e):
        high, low = split(source[e * 256 : (e + 1) * 256, :])
        rows = mm(left_mat[...], jnp.concatenate([high, high, low], axis=0))
        return rows + mm(jnp.concatenate([high, high, low], axis=1), right_mat[...])

    def store_inner(dest, source, e, value, scale):
        at = e * 256
        top, bottom = value[:PLANE], value[256 - PLANE :]
        if e > 0:
            top = top - scale * source[at - PLANE : at, :]
        if e < 3:
            bottom = bottom - scale * source[at + 256 : at + 256 + PLANE, :]
        dest[at : at + PLANE, :] = top
        dest[at + PLANE : at + 256 - PLANE, :] = value[PLANE : 256 - PLANE]
        dest[at + 256 - PLANE : at + 256, :] = bottom

    def expand(slot, opening, elements):
        src, dst = basis.at[slot], basis.at[slot + 1]
        for e in elements:
            rows = pl.ds(e * 256, 256)
            value = products(src, e) + (GAIN * mass[rows, :] - GAIN * CENTER) * src[rows, :]
            if opening:
                value = 0.5 * value
            else:
                value = value - basis[slot - 1, rows, :]
            store_inner(dst, src, e, value, pull * (0.5 if opening else 1.0))

    def outer(slot, side, plane, scale):
        at = sides[side][1]
        value = basis[slot, at : at + PLANE, :] - scale * plane
        basis[slot, at : at + PLANE, :] = value
        return value

    def along(plane, level, near_rows):
        high, low = split(plane)
        wide_plane = jnp.concatenate([high, high, low], axis=1)
        return near_rows + mm(wide_plane, right_mat[...]) + (GAIN * level - GAIN * CENTER) * plane

    def edge_map(side, plane):
        high, low = split(plane)
        rows = mm(edge_mat[...], jnp.concatenate([high, high, low], axis=0))
        return along(plane, first[side, 1], rows)

    def exchange_copies(ex):
        return [
            remote(stage.at[ex, side], ghost.at[ex, 1 - side], halo_s.at[ex, side], halo_r.at[ex, 1 - side], who)
            for side, _, _, who in sides
        ]

    def exchange_send(ex, slot):
        for side, at, place, _ in sides:
            e = 0 if side == 0 else 3
            high, low = split(basis[slot + 1, e * 256 : (e + 1) * 256, :])
            rows = mm(left_mat[place * PLANE : (place + 1) * PLANE, :], jnp.concatenate([high, high, low], axis=0))
            plane = basis[slot + 1, at : at + PLANE, :]
            own = basis[slot, at : at + PLANE, :]
            stage[ex, side, 0] = own
            stage[ex, side, 1] = plane
            stage[ex, side, 2] = along(plane, mass[at : at + PLANE, :], rows) - own
        for copy in exchange_copies(ex):
            copy.start()

    def exchange_wait(ex, slot, opening):
        for copy in exchange_copies(ex):
            copy.wait()
        scale = pull * (0.5 if opening else 1.0)
        for side, at, _, _ in sides:
            own = basis[slot, at : at + PLANE, :]
            then = outer(slot + 1, side, ghost[ex, side, 0], scale)
            beside[side, 0] = ghost[ex, side, 1] - scale * own
            beside[side, 1] = ghost[ex, side, 2] - scale * edge_map(side, own) - pull * then

    def follow(slot):
        for k in range(2):
            expand(slot + k, False, range(4))
            for side in range(2):
                outer(slot + k + 1, side, beside[side, k], pull)

    def accumulate(pairs, chunks):
        slots = sorted({a for _, a, _ in pairs} | {b for _, _, b in pairs})

        def body(c, carry):
            at = pl.multiple_of(c * 16, 16)
            rows = {s: basis[s, pl.ds(at, 16), :] for s in slots}
            return tuple(acc + fold(rows[a] * rows[b]) for acc, (_, a, b) in zip(carry, pairs))

        carry = tuple(jnp.zeros((8, 128), F32) for _ in pairs)
        carry = lax.fori_loop(0, chunks, body, carry, unroll=4)
        for (i, _, _), acc in zip(pairs, carry):
            dots[i] = acc

    stages = (
        (near, near_s, near_r, near_peer, near_me, GROUPS * LINE),
        (far, far_s, far_r, far_peer, sheet, SHEET),
    )

    def reduce_send(call, which, message):
        buffer, send, recv, peer, mine, n = stages[which]
        buffer[call, mine] = jnp.broadcast_to(message, (8, 128))
        own = buffer.at[call, mine]
        for o in range(1, n):
            remote(own, own, send.at[call, o], recv.at[call, mine], peer(o)[1]).start()

    def reduce_wait(call, which):
        buffer, send, recv, peer, mine, n = stages[which]
        own = buffer.at[call, mine]
        for o in range(1, n):
            other, who = peer(o)
            slot = buffer.at[call, other]
            remote(slot, slot, send.at[call, o], recv.at[call, other], who).wait_recv()
        for o in range(1, n):
            remote(own, own, send.at[call, o], recv.at[call, mine], peer(o)[1]).wait_send()
        total = buffer[call, 0]
        for i in range(1, n):
            total = total + buffer[call, i]
        return total

    def reduce_start(call, count):
        total = jnp.sum(dots[...], axis=1)
        column = jnp.sum(total, axis=1, keepdims=True)
        lane = lax.broadcasted_iota(jnp.int32, (24, 128), 1)
        place = lax.broadcasted_iota(jnp.int32, (24, 128), 0)
        keep = (lane == place) & (place < count)
        reduce_send(call, 0, jnp.sum(jnp.where(keep, column, 0.0), axis=0, keepdims=True))

    def reduce_middle(call):
        reduce_send(call, 1, reduce_wait(call, 0))

    def reduce_end(call, count):
        total = reduce_wait(call, 1)
        return [jnp.broadcast_to(total[:, i : i + 1], (8, 128)) for i in range(count)]

    def peer_copies(snap):
        block = table.at[snap, pl.ds(pl.multiple_of(me * 8, 8), 8)]
        return [remote(block, block, peer_s.at[snap], peer_r.at[snap], core_peer(grp, dom, o)) for o in range(1, DOMS)]

    def wait_peers(snap):
        arrived = table.at[snap, pl.ds(0, 8 * (DOMS - 1))]
        copy = remote(arrived, arrived, peer_s.at[snap], peer_r.at[snap], core_peer(grp, dom, 1))
        copy.wait_recv()
        copy.wait_send()

    def core_block(snap, which):
        return table.at[snap, pl.ds(pl.multiple_of(which * 512, 512), 512)]

    def core_copy(snap):
        block = core_block(snap, grp)
        return remote(block, block, core_s.at[snap], core_r.at[snap], other_core)

    def wait_core(snap):
        block = core_block(snap, 1 - grp)
        remote(block, block, core_s.at[snap], core_r.at[snap], other_core).wait_recv()
        core_copy(snap).wait_send()

    def start_all(copies):
        for copy in copies:
            copy.start()

    def write_to(ref):
        def write(i, row):
            ref[i : i + 1, :] = row

        return write

    def first_copies():
        return [
            remote(ref.at[pl.ds(at, PLANE)], first.at[1 - side, i], first_s.at[side, i], first_r.at[1 - side, i], who)
            for side, at, _, who in sides
            for i, ref in enumerate((vel, mass))
        ]

    for e in (0, 3, 1, 2):
        rows = pl.ds(e * 256, 256)
        store_inner(basis.at[0], vel, e, force[rows, :] - (1.0 / GAIN) * products(vel, e), -PENALTY)
    expand(0, True, (0, 3))
    pl.semaphore_wait(barrier, len(greeted))
    start_all(first_copies())
    exchange_send(0, 0)
    expand(0, True, (1, 2))
    onehot_rows(sample, hot_sample)
    keys[...] = jnp.where(valid[...] != 0, source[...] * NODES + target_node[...], NODES * NODES)
    for copy in first_copies():
        copy.wait()
    for side in range(2):
        outer(0, side, first[side, 0], -PENALTY)
    expand(0, True, (0, 3))
    for copy in exchange_copies(0):
        copy.wait()
    for side, at, _, _ in sides:
        own = basis[0, at : at + PLANE, :]
        given = PENALTY * vel[at : at + PLANE, :]
        mapped = edge_map(side, given)
        then = outer(1, side, ghost[0, side, 0] + given, 0.5 * pull)
        beside[side, 0] = ghost[0, side, 1] + 0.5 * mapped - (0.5 * pull) * own
        beside[side, 1] = (
            ghost[0, side, 2] + 0.5 * edge_map(side, mapped - pull * own) + (0.5 * REACH - 1.0) * given - pull * then
        )

    for step in range(STEPS):
        call = 2 * step
        if step > 0:
            expand(0, True, (0, 3))
            exchange_send(2 * step, 0)
            expand(0, True, (1, 2))
            picked = []
            pick(out[...], sample, hot_sample, lambda i, row: picked.append(row))
            table[step - 1, pl.ds(pl.multiple_of(me * 8, 8), 8), :] = jnp.concatenate(picked, axis=0)
            start_all(peer_copies(step - 1))
            exchange_wait(2 * step, 0, True)
        follow(1)
        index = {}
        for j in range(4):
            for i in range(min(j, 2) + 1):
                index[i, j] = index[j, i] = len(index) - sum(1 for a, b in index if a > b)
        accumulate([(n, i, j) for (i, j), n in index.items() if i <= j], 64)
        reduce_start(call, 9)
        expand(3, False, (0, 3))
        exchange_send(2 * step + 1, 3)
        expand(3, False, (1, 2))
        reduce_middle(call)
        if step == 0:
            onehot_rows(part, hot_part)
        exchange_wait(2 * step + 1, 3, False)
        follow(4)
        m = reduce_end(call, 9)
        gram = [[m[index[i, j]] for j in range(3)] for i in range(4)]
        image = image_rows(gram, 3)
        head = [[image[max(i, j)][min(i, j)] for j in range(3)] for i in range(3)]
        opening = solve(head, gram[0])
        after_three = [-c for c in image_coefs(opening)]
        after_three[0] = 1.0 + after_three[0]
        combos = [after_three, shifted(after_three)]
        for _ in range(2):
            combos.append([2.0 * c for c in shifted(combos[-1])])
            for i, c in enumerate(combos[-3]):
                combos[-1][i] = combos[-1][i] - c
        factors = [[wide(c) for c in coefs] for coefs in combos]
        pairs = [(i, 4 + j) for j in range(3) for i in range(4)]
        pairs += [(4 + i, 4 + j) for j in range(4) for i in range(min(j, 2) + 1)]

        def gather_dots(c, carry):
            at = pl.multiple_of(c * 16, 16)
            rows = [basis[s, pl.ds(at, 16), :] for s in range(7)]
            for coefs in factors:
                value = coefs[0] * rows[0]
                for c_i, row in zip(coefs[1:], rows[1:7]):
                    value = value + c_i * row
                rows.append(value)
            held = rows[:4] + rows[7:]
            return tuple(acc + fold(held[a] * held[b]) for acc, (a, b) in zip(carry, pairs))

        carry = lax.fori_loop(0, 64, gather_dots, tuple(jnp.zeros((8, 128), F32) for _ in pairs))
        for i, acc in enumerate(carry):
            dots[i] = acc
        reduce_start(call + 1, len(pairs))
        if step > 0:
            wait_peers(step - 1)
            core_copy(step - 1).start()
        reduce_middle(call + 1)
        if step > 0:
            wait_core(step - 1)
            pick(table[step - 1], part, hot_part, write_to(feats))
        m = reduce_end(call + 1, len(pairs))
        index = {}
        for n, (a, b) in enumerate(pairs):
            index[a, b] = index[b, a] = n
        cross = image_rows([[m[index[i, 4 + j]] for j in range(3)] for i in range(4)], 3)
        gram = [[m[index[4 + i, 4 + j]] for j in range(3)] for i in range(4)]
        image = image_rows(gram, 3)
        whole = [[None] * 6 for _ in range(6)]
        for i in range(3):
            for j in range(3):
                whole[i][j] = head[i][j]
                whole[3 + i][3 + j] = image[max(i, j)][min(i, j)]
                whole[i][3 + j] = whole[3 + j][i] = cross[i][j]
        coefs = solve(whole, [m[index[i, 4]] for i in range(3)] + gram[0])
        moves = merged([(None, opening), (None, coefs[:3])] + [(coefs[3 + j], combos[j]) for j in range(3)])
        lost = image_coefs(coefs[3:])
        rest = merged([(None, combos[0])] + [(-lost[j], combos[j]) for j in range(4)] + [(-1.0, image_coefs(coefs[:3]))])
        moves = [wide(c) for c in moves]
        rest = [wide(c) for c in rest]
        start = vel if step == 0 else out
        more = step < STEPS - 1

        def advance(c, carry):
            rows = pl.ds(pl.multiple_of(c * 16, 16), 16)
            held = [basis[s, rows, :] for s in range(7 if more else 6)]
            moved = moves[0] * held[0]
            for c_i, row in zip(moves[1:], held[1:]):
                moved = moved + c_i * row
            if more:
                value = mass[rows, :] * moved
                for c_i, row in zip(rest, held):
                    value = value + c_i * row
                basis[0, rows, :] = value
            out[rows, :] = start[rows, :] + moved
            return carry

        lax.fori_loop(0, 64, advance, 0, unroll=2)

    last = STEPS - 1
    picked = []
    pick(out[...], sample, hot_sample, lambda i, row: picked.append(row))
    table[last, pl.ds(pl.multiple_of(me * 8, 8), 8), :] = jnp.concatenate(picked, axis=0)
    start_all(peer_copies(last))
    wait_peers(last)
    core_copy(last).start()
    here, there = (pl.ds(pl.multiple_of(which * 512, 512), 512) for which in (grp, 1 - grp))
    pick(table[last, here, :], part, hot_part.at[here], write_to(target))
    wait_core(last)

    def add_to(i, row):
        target[i : i + 1, :] = target[i : i + 1, :] + row

    pick(table[last, there, :], part, hot_part.at[there], add_to)


VMEM = pl.BlockSpec(memory_space=pltpu.VMEM)
SMEM = pl.BlockSpec(memory_space=pltpu.SMEM)
ANY = pl.BlockSpec(memory_space=pl.ANY)


def run_steps(velocity, forcing, mass, sample, part, source, target_node, valid):
    dma = pltpu.SemaphoreType.DMA
    return pl.pallas_call(
        steps_kernel,
        out_shape=(
            jax.ShapeDtypeStruct((ROWS, 256), F32),
            jax.ShapeDtypeStruct((8, 256), F32),
            jax.ShapeDtypeStruct((8, 256), F32),
            jax.ShapeDtypeStruct((64, 128), jnp.int32),
        ),
        in_specs=[VMEM] * 11,
        out_specs=(VMEM,) * 4,
        scratch_shapes=[
            pltpu.VMEM((7, ROWS, 256), F32),
            pltpu.VMEM((4, 2, 3, PLANE, 256), F32),
            pltpu.VMEM((4, 2, 3, PLANE, 256), F32),
            pltpu.VMEM((2, 2, PLANE, 256), F32),
            pltpu.VMEM((2, 2, PLANE, 256), F32),
            pltpu.VMEM((24, 8, 128), F32),
            pltpu.VMEM((4, 8, 8, 128), F32),
            pltpu.VMEM((4, 16, 8, 128), F32),
            pltpu.VMEM((2, ROWS, 256), F32),
            pltpu.VMEM((ROWS, NODES), BF16),
            pltpu.VMEM((ROWS, NODES), BF16),
            dma((4, 2)), dma((4, 2)),
            dma((2, 2)), dma((2, 2)),
            dma((4, 8)), dma((4, 8)),
            dma((4, 16)), dma((4, 16)),
            dma((2,)), dma((2,)),
            dma((2,)), dma((2,)),
        ],
        compiler_params=pltpu.CompilerParams(
            collective_id=0, has_side_effects=True, vmem_limit_bytes=56 << 20
        ),
        cost_estimate=pl.CostEstimate(flops=30_000_000_000, bytes_accessed=4 << 20, transcendentals=0),
        name="viscous_steps",
    )(velocity, forcing, mass, sample, part, source, target_node, valid, *field_matrices())


def split3(value, axis):
    high, low = split(value)
    return jnp.concatenate([high, high, low], axis=axis)


def split3_other(value, axis):
    high, low = split(value)
    return jnp.concatenate([high, low, high], axis=axis)


HALF_PAGES = 8
COUNT_ROWS = HALF_PAGES * NODES


def count_edges(key_ref, adj, accs):
    def clear(i, carry):
        for acc in accs:
            acc[pl.ds(pl.multiple_of(i * 128, 128), 128), :] = jnp.zeros((128, 128), jnp.int32)
        return carry

    lax.fori_loop(0, COUNT_ROWS // 128, clear, 0)
    place = lax.broadcasted_iota(jnp.int32, (8, 128), 0) * 128 + lax.broadcasted_iota(jnp.int32, (8, 128), 1)
    stream = EDGES // len(accs)

    def add(i, carry):
        for u in range(8):
            keys = [key_ref[c * stream + i * 8 + u] for c in range(len(accs))]
            spots = [pl.ds(pl.multiple_of((k >> 11) * 8, 8), 8) for k in keys]
            held = [acc[spot, :] for acc, spot in zip(accs, spots)]
            for acc, spot, k, value in zip(accs, spots, keys, held):
                word = jnp.full((8, 128), k, jnp.int32)
                one = lax.shift_left(jnp.full((8, 128), 1, jnp.int32), (word >> 6) & 16)
                acc[spot, :] = value + jnp.where((word & 1023) == place, one, 0)
        return carry

    lax.fori_loop(0, stream // 8, add, 0)

    def total(i, carry):
        rows = pl.ds(pl.multiple_of(i * 128, 128), 128)
        value = accs[0][rows, :]
        for acc in accs[1:]:
            value = value + acc[rows, :]
        accs[0][rows, :] = value
        return carry

    lax.fori_loop(0, COUNT_ROWS // 128, total, 0, unroll=2)

    def halves(rows):
        value = accs[0][rows, :]
        return (value & 65535).astype(F32), (value >> 16).astype(F32)

    worst = jnp.zeros((128, 128), F32)
    for page in range(HALF_PAGES):

        def move(i, most):
            at = pl.multiple_of(i * 128, 128)
            for h, value in enumerate(halves(page_rows(at, page, 128))):
                low = value.astype(BF16)
                column = h * 1024 + page * 128
                adj[pl.ds(at, 128), column : column + 128] = low
                most = jnp.maximum(most, jnp.abs(value - low.astype(F32)))
            return most

        worst = lax.fori_loop(0, NODES // 128, move, worst, unroll=2)
    flagged = jnp.max(worst) > 0.0

    @pl.when(flagged)
    def _():
        def keep(i, carry):
            rows = pl.ds(pl.multiple_of(i * 128, 128), 128)
            for acc, value in zip(accs, halves(rows)):
                acc[rows, :] = (value - value.astype(BF16).astype(F32)).astype(jnp.int32)
            return carry

        lax.fori_loop(0, COUNT_ROWS // 128, keep, 0)

    return flagged


def page_rows(start, page, count):
    return pl.ds(start * 8 + page, count, stride=8)


def surrogate_kernel(
    key_ref, feats, target, w_in_ref, b_in_ref, bias_ref, w_out_ref, weights, field,
    out, field_out,
    one, two, three, four, adj, feat_row, target_row, state_0, state_1, agg_0, agg_1, slope_0, slope_1, partial_0, partial_1,
    sent_0, sent_1, sent_2, sent_3, back_agg, extra, grads_0, grads_1, w_fwd, w_bwd, field_hold, sem,
):
    tiles = NODES // 256
    states, aggs, slopes, partials = (state_0, state_1), (agg_0, agg_1), (slope_0, slope_1), (partial_0, partial_1)
    sent, grads = (sent_0, sent_1, sent_2, sent_3), (grads_0, grads_1)
    field_in = pltpu.make_async_copy(field, field_hold, sem.at[0])
    field_in.start()
    accs = (one, two, three, four)
    flagged = count_edges(key_ref, adj, accs)
    field_in.wait()
    field_back = pltpu.make_async_copy(field_hold, field_out, sem.at[1])
    field_back.start()
    for i in range(8):
        feat_row[:, i * 256 : (i + 1) * 256] = feats[i : i + 1, :]
        target_row[:, i * 256 : (i + 1) * 256] = target[i : i + 1, :]
    vectors = [w_in_ref[...], b_in_ref[...], bias_ref[...], w_out_ref[...], jnp.zeros((123, 128), F32)]
    columns = jnp.concatenate(vectors, axis=0).T
    w_in, b_in, w_out = columns[:, 0:1], columns[:, 1:2], columns[:, 4:5]
    biases = (columns[:, 2:3], columns[:, 3:4])
    for layer in range(LAYERS):
        weight = weights[layer]
        w_fwd[layer] = split3_other(weight.T, 1)
        w_bwd[layer] = split3_other(weight, 1)
    for ref in grads:
        ref[...] = jnp.zeros_like(ref)
    extra[...] = jnp.zeros_like(extra)

    def lanes(j):
        return pl.ds(pl.multiple_of(j * 256, 256), 256)

    def send(slot, at, value):
        high, low = split(value)
        sent[slot][0:128, at] = high
        sent[slot][128:256, at] = low

    def both(rows):
        return rows[:128] + rows[128:]

    def spill(half, rows):
        return accs[half][rows, :].astype(F32).astype(BF16)

    def gather_extra(slot):
        @pl.when(flagged)
        def _():
            for half in range(2):

                def body(page, carry):
                    rows = both(mm(sent[slot][...], spill(half, page_rows(0, page, NODES))))
                    extra[:, pl.ds(pl.multiple_of(half * 1024 + page * 128, 128), 128)] = rows
                    return carry

                lax.fori_loop(0, HALF_PAGES, body, 0)

    def scatter_extra(slot):
        @pl.when(flagged)
        def _():
            def body(j, carry):
                rows = jnp.zeros((256, 256), F32)
                for half in range(2):
                    for page in range(HALF_PAGES):
                        column = half * 1024 + page * 128
                        block = spill(half, page_rows(j * 256, page, 256))
                        rows = rows + mm_lanes(sent[slot][:, column : column + 128], block)
                extra[:, lanes(j)] = both(rows)
                return carry

            lax.fori_loop(0, tiles, body, 0)

    def gather(slot, into):
        gather_extra(slot)

        def body(j, carry):
            at = lanes(j)
            into[:, at] = AGG_SCALE * (both(mm(sent[slot][...], adj[:, at])) + extra[:, at])
            return carry

        lax.fori_loop(0, tiles, body, 0, unroll=8)

    def scatter(slot):
        scatter_extra(slot)

        def body(j, carry):
            at = lanes(j)
            back_agg[:, at] = AGG_SCALE * (both(mm_lanes(sent[slot][...], adj[at, :])) + extra[:, at])
            return carry

        lax.fori_loop(0, tiles, body, 0, unroll=8)

    def opening(j, carry):
        at = lanes(j)
        value = jnp.tanh(w_in * feat_row[:, at] + b_in)
        states[0][:, at] = value
        send(0, at, value)
        return carry

    lax.fori_loop(0, tiles, opening, 0, unroll=2)

    def joined(layer, at):
        return jnp.concatenate([states[layer][:, at], aggs[layer][:, at]], axis=0)

    def update(layer, at):
        bump = jnp.tanh(mm(w_fwd[layer], split3(joined(layer, at), 0)) + biases[layer])
        slopes[layer][:, at] = 1.0 - bump * bump
        return states[layer][:, at] + bump

    def back(layer, at, above):
        pre = above * slopes[layer][:, at]
        grads[layer][...] = grads[layer][...] + mm_lanes(split3(joined(layer, at), 1), split3_other(pre, 1))
        below = mm(w_bwd[layer], split3(pre, 0))
        partials[layer][:, at] = above + below[:128]
        send(2 + layer, at, below[128:])
        return jnp.sum(pre, axis=1, keepdims=True)

    def second(j, carry):
        at = lanes(j)
        value = update(0, at)
        states[1][:, at] = value
        send(1, at, value)
        return carry

    gather(0, agg_0)
    lax.fori_loop(0, tiles, second, 0, unroll=8)

    zero = jnp.zeros((128, 1), F32)

    def third(j, carry):
        loss, grad_out, grad_bias = carry
        at = lanes(j)
        value = update(1, at)
        miss = jnp.sum(w_out * value, axis=0, keepdims=True) - target_row[:, at]
        scaled = miss * (2.0 / (NODES * GROUPS * DOMS))
        loss = loss + miss * miss
        grad_out = grad_out + jnp.sum(value * scaled, axis=1, keepdims=True)
        return loss, grad_out, grad_bias + back(1, at, w_out * scaled)

    gather(1, agg_1)
    loss, grad_out, bias_1 = lax.fori_loop(
        0, tiles, third, (jnp.zeros((1, 256), F32), zero, zero), unroll=8
    )

    def fourth(j, carry):
        at = lanes(j)
        return carry + back(0, at, partials[1][:, at] + back_agg[:, at])

    scatter(3)
    bias_0 = lax.fori_loop(0, tiles, fourth, zero, unroll=8)

    def fifth(j, carry):
        grad_in, grad_bias = carry
        at = lanes(j)
        value = states[0][:, at]
        pre = (partials[0][:, at] + back_agg[:, at]) * (1.0 - value * value)
        grad_in = grad_in + jnp.sum(pre * feat_row[:, at], axis=1, keepdims=True)
        return grad_in, grad_bias + jnp.sum(pre, axis=1, keepdims=True)

    scatter(2)
    grad_in, grad_bias = lax.fori_loop(0, tiles, fifth, (zero, zero), unroll=8)
    loss = jnp.sum(loss, axis=1, keepdims=True) * (1.0 / (NODES * GROUPS * DOMS))
    lane = lax.broadcasted_iota(jnp.int32, (128, 128), 1)
    packed = jnp.where(lane == 5, loss, 0.0)
    for i, column in enumerate((grad_in, grad_bias, bias_0, bias_1, grad_out)):
        packed = packed + jnp.where(lane == i, column, 0.0)
    blank = jnp.zeros((3, 128), F32)
    for f in range(128):
        out[f, 0:4, :] = grads[f // 64][f % 64 * 4 : f % 64 * 4 + 4, :]
        out[f, 4:5, :] = packed[f : f + 1, :]
        out[f, 5:8, :] = blank
    field_back.wait()


def surrogate(key, feats, target, w_in, b_in, layer_bias, w_out, layer_weights, field):
    return pl.pallas_call(
        surrogate_kernel,
        out_shape=(jax.ShapeDtypeStruct((128, 8, 128), F32), jax.ShapeDtypeStruct((ROWS, 256), F32)),
        in_specs=[SMEM] + [VMEM] * 7 + [ANY],
        out_specs=(VMEM, ANY),
        scratch_shapes=[pltpu.VMEM((COUNT_ROWS + 8, 128), jnp.int32)] * 4
        + [
            pltpu.VMEM((NODES, NODES), BF16),
            pltpu.VMEM((1, NODES), F32),
            pltpu.VMEM((1, NODES), F32),
        ]
        + [pltpu.VMEM((128, NODES), F32)] * 8
        + [pltpu.VMEM((256, NODES), BF16)] * 4
        + [pltpu.VMEM((128, NODES), F32)] * 2
        + [pltpu.VMEM((256, 128), F32)] * 2
        + [
            pltpu.VMEM((LAYERS, 128, 768), BF16),
            pltpu.VMEM((LAYERS, 256, 384), BF16),
            pltpu.VMEM((ROWS, 256), F32),
            pltpu.SemaphoreType.DMA((2,)),
        ],
        compiler_params=pltpu.CompilerParams(vmem_limit_bytes=62 << 20),
        name="surrogate",
    )(
        key, feats, target, w_in.reshape(1, 128), b_in.reshape(1, 128), layer_bias, w_out.reshape(1, 128),
        layer_weights, field,
    )


def sum_kernel(
    grads, out, other, total, share, result, core_s, core_r, share_s, share_r, back_s, back_r, last_s, last_r
):
    grp = lax.axis_index("grp")
    dom = lax.axis_index("dom")
    other_core = (1 - grp, dom)
    peers = [core_peer(grp, dom, o) for o in range(1, DOMS)]

    def remote(src, dst, send, recv, who):
        return pltpu.make_async_remote_copy(
            src_ref=src, dst_ref=dst, send_sem=send, recv_sem=recv, device_id=who, device_id_type=MESH
        )

    barrier = pltpu.get_barrier_semaphore()
    for who in peers + [other_core]:
        pl.semaphore_signal(barrier, inc=1, device_id=who, device_id_type=MESH)
    pl.semaphore_wait(barrier, DOMS)

    def half(which):
        return pl.ds(pl.multiple_of(which * DOMS, DOMS), DOMS)

    copy = remote(grads.at[half(1 - grp)], other, core_s, core_r, other_core)
    copy.start()
    copy.wait()
    total[...] = grads[half(grp)] + other[...]
    for _, peer in peers:
        remote(total.at[peer], share.at[dom], share_s, share_r, (grp, peer)).start()
    share[dom] = total[dom]
    arrived = share.at[pl.ds(0, DOMS - 1)]
    copy = remote(arrived, arrived, share_s, share_r, peers[0])
    copy.wait_recv()
    copy.wait_send()
    parts = [share[i] for i in range(DOMS)]
    while len(parts) > 1:
        parts = [a + b for a, b in zip(parts[::2], parts[1::2])]
    mine = grp * DOMS + dom
    result[mine] = parts[0]
    for who in peers:
        remote(result.at[mine], result.at[mine], back_s, back_r, who).start()
    arrived = result.at[pl.ds(0, DOMS - 1)]
    copy = remote(arrived, arrived, back_s, back_r, peers[0])
    copy.wait_recv()
    copy.wait_send()
    own = result.at[half(grp)]
    copy = remote(own, own, last_s, last_r, other_core)
    copy.start()
    out[half(grp)] = result[half(grp)]
    there = result.at[half(1 - grp)]
    remote(there, there, last_s, last_r, other_core).wait_recv()
    out[half(1 - grp)] = result[half(1 - grp)]
    copy.wait_send()


def sum_grads(grads):
    dma = pltpu.SemaphoreType.DMA
    return pl.pallas_call(
        sum_kernel,
        out_shape=jax.ShapeDtypeStruct((128, 8, 128), F32),
        in_specs=[VMEM],
        out_specs=VMEM,
        scratch_shapes=[
            pltpu.VMEM((DOMS, 8, 128), F32),
            pltpu.VMEM((DOMS, 8, 128), F32),
            pltpu.VMEM((DOMS, 8, 128), F32),
            pltpu.VMEM((2 * DOMS, 8, 128), F32),
        ]
        + [dma] * 8,
        compiler_params=pltpu.CompilerParams(collective_id=1, has_side_effects=True, vmem_limit_bytes=32 << 20),
        name="sum_grads",
    )(grads)


def unpack_kernel(tiles, weight_out, in_out, bias_in_out, bias_out, head_out, loss_out):
    for f in range(128):
        weight_out[f // 64, f % 64 * 4 : f % 64 * 4 + 4, :] = tiles[f, 0:4, :]
    rows = tiles[:, 4, :].T
    in_out[...] = rows[0:1, :]
    bias_in_out[...] = rows[1:2, :]
    bias_out[...] = rows[2:4, :]
    head_out[...] = rows[4:5, :]
    loss_out[...] = rows[5:6, 0:1]


def unpack(tiles):
    row = jax.ShapeDtypeStruct((1, 128), F32)
    return pl.pallas_call(
        unpack_kernel,
        out_shape=(
            jax.ShapeDtypeStruct((LAYERS, 256, 128), F32), row, row, jax.ShapeDtypeStruct((2, 128), F32), row,
            jax.ShapeDtypeStruct((1, 1), F32),
        ),
        in_specs=[VMEM],
        out_specs=(VMEM,) * 6,
        name="unpack",
    )(tiles)


def shards(
    velocity, forcing, mass, sample_index, partition, edge_source, edge_target, edge_valid,
    w_in, b_in, layer_weights, layer_bias, w_out,
):
    shape = velocity.shape
    field, feats, target, keys = run_steps(
        velocity.reshape(ROWS, 256), forcing.reshape(ROWS, 256), mass.reshape(ROWS, 256),
        sample_index.reshape(16, 128), partition.reshape(16, 128),
        edge_source.reshape(64, 128), edge_target.reshape(64, 128), edge_valid.reshape(64, 128),
    )
    grads, field = surrogate(
        keys.reshape(EDGES), feats, target, w_in, b_in, layer_bias, w_out, layer_weights, field,
    )
    weight, grad_in, grad_bin, bias, head, loss = unpack(sum_grads(grads))
    return (
        field.reshape(shape), loss.reshape(()), grad_in.reshape(128), grad_bin.reshape(128), weight, bias,
        head.reshape(128),
    )


def solution(mesh):
    many = P(("grp", "dom"))
    block = P(("grp", "dom"), None, None)
    return jax.shard_map(
        shards,
        mesh=mesh,
        in_specs=(block,) * 3 + (many,) * 5 + (P(),) * 5,
        out_specs=(block,) + (P(),) * 6,
        check_vma=False,
    )
```

```python
import functools

import jax
import jax.numpy as jnp
import ml_dtypes
import numpy as np
from jax import lax
from jax.experimental import pallas as pl
from jax.experimental.pallas import tpu as pltpu
from jax.sharding import PartitionSpec as P

MESH = pl.DeviceIdType.MESH
F32 = jnp.float32
BF16 = jnp.bfloat16

STEPS = 2
LAYERS = 2
PENALTY = 2.0
AGG_SCALE = 0.25
NODES = 2048
EDGES = 8192
ROWS = 1024
PLANE = 32
GROUPS, DOMS, LINE, SHEET = 2, 64, 4, 16

CENTER = 14.125
HALF = 12.575
GAIN = 2.0 / HALF
PIVOT = 1e-6
REACH = GAIN * GAIN * float(sum(np.exp(-2.0 * i) for i in range(1, 8)))
CHIP_ORDER = [0] + sorted(
    range(1, DOMS), key=lambda o: -sum(min(c, 4 - c) for c in (o % 4, o // 4 % 4, o // 16))
)
FAR_ORDER = [0] + sorted(range(1, 16), key=lambda o: -(min(o % 4, 4 - o % 4) + min(o // 4, 4 - o // 4)))


def split_np(matrix):
    high = matrix.astype(np.float32).astype(ml_dtypes.bfloat16)
    low = (matrix - high.astype(np.float64)).astype(np.float32).astype(ml_dtypes.bfloat16)
    return high, low


def element_matrix():
    at = np.arange(8)
    return 2.5 * np.eye(8) - np.exp(-np.abs(at[:, None] - at[None, :]).astype(np.float64))


def line_matrix(length, wrap):
    matrix = np.kron(np.eye(length // 8), element_matrix())
    for last in range(7, length, 8):
        follow = (last + 1) % length
        if follow == 0 and not wrap:
            continue
        matrix[last, last] += PENALTY
        matrix[follow, follow] += PENALTY
        matrix[last, follow] -= PENALTY
        matrix[follow, last] -= PENALTY
    return matrix


def field_matrices():
    ends = np.zeros(8)
    ends[0] = ends[7] = PENALTY
    sheet = np.kron(element_matrix() + np.diag(ends), np.eye(32)) + np.kron(np.eye(8), line_matrix(32, False))
    sheet_high, sheet_low = split_np(GAIN * sheet)
    span_high, span_low = split_np(GAIN * line_matrix(256, True))
    left = np.concatenate([sheet_high, sheet_low, sheet_high], axis=1)
    right = np.concatenate([span_high, span_low, span_high], axis=0)
    edge = np.concatenate([sheet_high[:32, :32], sheet_low[:32, :32], sheet_high[:32, :32]], axis=1)
    return left, right, edge


def split(value):
    high = value.astype(BF16)
    return high, (value - high.astype(F32)).astype(BF16)


def mm(left, right):
    return jnp.dot(left, right, preferred_element_type=F32)


def mm_lanes(left, right):
    return lax.dot_general(left, right, (((1,), (1,)), ((), ())), preferred_element_type=F32)


def wide(tile):
    two = jnp.concatenate([tile, tile], axis=1)
    return jnp.concatenate([two, two], axis=0)


def fold(value):
    half = value[:8] + value[8:]
    return half[:, :128] + half[:, 128:]


def solve(matrix, rhs):
    n = len(rhs)
    rows = [list(row) for row in matrix]
    right = list(rhs)
    lower = {}
    inverse = []
    for k in range(n):
        pivot = rows[k][k]
        inverse.append(jnp.where(pivot > PIVOT * matrix[k][k], 1.0 / pivot, 0.0))
        for i in range(k + 1, n):
            factor = rows[k][i] * inverse[k]
            lower[i, k] = factor
            for j in range(i, n):
                rows[i][j] = rows[i][j] - factor * rows[k][j]
            right[i] = right[i] - factor * right[k]
    out = [None] * n
    for k in reversed(range(n)):
        value = right[k] * inverse[k]
        for i in range(k + 1, n):
            value = value - lower[i, k] * out[i]
        out[k] = value
    return out


def image_rows(gram, count):
    out = []
    for i in range(count):
        out.append(
            [CENTER * a + (0.5 * HALF) * (b + c) for a, b, c in zip(gram[i], gram[i + 1], gram[abs(i - 1)])]
        )
    return out


def image_coefs(coefs):
    out = [None] * (len(coefs) + 1)

    def add(at, value):
        out[at] = value if out[at] is None else out[at] + value

    for j, c in enumerate(coefs):
        add(j, CENTER * c)
        if j == 0:
            add(1, HALF * c)
        else:
            add(j + 1, (0.5 * HALF) * c)
            add(j - 1, (0.5 * HALF) * c)
    return out


def index_row(index_ref, i):
    return jnp.concatenate([index_ref[2 * i : 2 * i + 1, :], index_ref[2 * i + 1 : 2 * i + 2, :]], axis=1)


def onehot_rows(index_ref, out_ref):
    for i in range(8):
        row = index_row(index_ref, i) >> 8

        def body(c, carry):
            at = pl.multiple_of(c * 128, 128)
            place = lax.broadcasted_iota(jnp.int32, (128, 256), 0) + at
            out_ref[pl.ds(at, 128), i * 256 : (i + 1) * 256] = jnp.where(place == row, 1.0, 0.0).astype(BF16)
            return carry

        lax.fori_loop(0, ROWS // 128, body, 0)


def pick(table, index_ref, onehot_ref, write):
    both = jnp.concatenate(split(table.T), axis=0)
    place = lax.broadcasted_iota(jnp.int32, (256, 256), 0)
    for i in range(8):
        rows = mm(both, onehot_ref[:, i * 256 : (i + 1) * 256])
        rows = rows[:256] + rows[256:]
        column = index_row(index_ref, i) & 255
        write(i, jnp.sum(jnp.where(place == column, rows, 0.0), axis=0, keepdims=True))


def shifted(coefs):
    out = [None] * (len(coefs) + 1)

    def add(at, value):
        out[at] = value if out[at] is None else out[at] + value

    for i, c in enumerate(coefs):
        if i == 0:
            add(1, c)
        else:
            add(i + 1, 0.5 * c)
            add(i - 1, 0.5 * c)
    return out


def merged(parts):
    out = []
    for factor, coefs in parts:
        for i, c in enumerate(coefs):
            value = c if factor is None else factor * c
            if i < len(out):
                out[i] = out[i] + value
            else:
                out.append(value)
    return out


def core_peer(grp, dom, o):
    hop = CHIP_ORDER[o]
    y, z, x = (dom // 16 + hop // 16) % 4, (dom // 4 + hop // 4) % 4, (dom + hop) % 4
    return grp, y * 16 + z * 4 + x


def steps_kernel(
    vel, force_hbm, mass_hbm, sample, part, source, target_node, valid, left_mat, right_mat, edge_mat,
    out_hbm, feats, target, keys,
    force, mass, out, local, basis, stage, ghost, first, beside, dots, near, far, table, hot_sample, hot_part,
    halo_s, halo_r, first_s, first_r, near_s, near_r, far_s, far_r, peer_s, peer_r, core_s, core_r,
):
    grp = lax.axis_index("grp")
    dom = lax.axis_index("dom")
    me = grp * DOMS + dom
    line = dom % LINE
    sheet = dom // LINE
    near_me = grp * LINE + line

    def near_peer(o):
        other = (near_me + o) % (GROUPS * LINE)
        return other, (other // LINE, sheet * LINE + other % LINE)

    def far_peer(o):
        hop = FAR_ORDER[o]
        other = (sheet // 4 + hop // 4) % 4 * 4 + (sheet + hop) % 4
        return other, (grp, other * LINE + line)

    other_core = (1 - grp, dom)
    after = (me + 1) % (GROUPS * DOMS)
    before = (me + GROUPS * DOMS - 1) % (GROUPS * DOMS)
    after_id = (after // DOMS, after % DOMS)
    before_id = (before // DOMS, before % DOMS)

    loads = [
        pltpu.make_async_copy(force_hbm, force, local.at[0]),
        pltpu.make_async_copy(mass_hbm, mass, local.at[1]),
    ]
    for copy in loads:
        copy.start()
    barrier = pltpu.get_barrier_semaphore()
    greeted = [core_peer(grp, dom, o) for o in range(1, DOMS)] + [near_peer(o)[1] for o in range(1, 8)]
    greeted += [after_id, before_id]
    for who in greeted:
        pl.semaphore_signal(barrier, inc=1, device_id=who, device_id_type=MESH)

    def remote(src, dst, send, recv, who):
        return pltpu.make_async_remote_copy(
            src_ref=src, dst_ref=dst, send_sem=send, recv_sem=recv, device_id=who, device_id_type=MESH
        )

    sides = ((0, 0, 0, before_id), (1, ROWS - PLANE, 7, after_id))
    pull = PENALTY * GAIN

    def products(source, e):
        high, low = split(source[e * 256 : (e + 1) * 256, :])
        rows = mm(left_mat[...], jnp.concatenate([high, high, low], axis=0))
        return rows + mm(jnp.concatenate([high, high, low], axis=1), right_mat[...])

    def store_inner(dest, source, e, value, scale):
        at = e * 256
        top, bottom = value[:PLANE], value[256 - PLANE :]
        if e > 0:
            top = top - scale * source[at - PLANE : at, :]
        if e < 3:
            bottom = bottom - scale * source[at + 256 : at + 256 + PLANE, :]
        dest[at : at + PLANE, :] = top
        dest[at + PLANE : at + 256 - PLANE, :] = value[PLANE : 256 - PLANE]
        dest[at + 256 - PLANE : at + 256, :] = bottom

    def expand(slot, opening, elements):
        src, dst = basis.at[slot], basis.at[slot + 1]
        for e in elements:
            rows = pl.ds(e * 256, 256)
            value = products(src, e) + (GAIN * mass[rows, :] - GAIN * CENTER) * src[rows, :]
            if opening:
                value = 0.5 * value
            else:
                value = value - basis[slot - 1, rows, :]
            store_inner(dst, src, e, value, pull * (0.5 if opening else 1.0))

    def outer(slot, side, plane, scale):
        at = sides[side][1]
        value = basis[slot, at : at + PLANE, :] - scale * plane
        basis[slot, at : at + PLANE, :] = value
        return value

    def along(plane, level, near_rows):
        high, low = split(plane)
        wide_plane = jnp.concatenate([high, high, low], axis=1)
        return near_rows + mm(wide_plane, right_mat[...]) + (GAIN * level - GAIN * CENTER) * plane

    def edge_map(side, plane):
        high, low = split(plane)
        rows = mm(edge_mat[...], jnp.concatenate([high, high, low], axis=0))
        return along(plane, first[side, 1], rows)

    def exchange_copies(ex):
        return [
            remote(stage.at[ex, side], ghost.at[ex, 1 - side], halo_s.at[ex, side], halo_r.at[ex, 1 - side], who)
            for side, _, _, who in sides
        ]

    def exchange_send(ex, slot):
        for side, at, place, _ in sides:
            e = 0 if side == 0 else 3
            high, low = split(basis[slot + 1, e * 256 : (e + 1) * 256, :])
            rows = mm(left_mat[place * PLANE : (place + 1) * PLANE, :], jnp.concatenate([high, high, low], axis=0))
            plane = basis[slot + 1, at : at + PLANE, :]
            own = basis[slot, at : at + PLANE, :]
            stage[ex, side, 0] = own
            stage[ex, side, 1] = plane
            stage[ex, side, 2] = along(plane, mass[at : at + PLANE, :], rows) - own
        for copy in exchange_copies(ex):
            copy.start()

    def exchange_wait(ex, slot, opening):
        for copy in exchange_copies(ex):
            copy.wait()
        scale = pull * (0.5 if opening else 1.0)
        for side, at, _, _ in sides:
            own = basis[slot, at : at + PLANE, :]
            then = outer(slot + 1, side, ghost[ex, side, 0], scale)
            beside[side, 0] = ghost[ex, side, 1] - scale * own
            beside[side, 1] = ghost[ex, side, 2] - scale * edge_map(side, own) - pull * then

    def follow(slot):
        for k in range(2):
            expand(slot + k, False, range(4))
            for side in range(2):
                outer(slot + k + 1, side, beside[side, k], pull)

    def accumulate(pairs, chunks):
        slots = sorted({a for _, a, _ in pairs} | {b for _, _, b in pairs})

        def body(c, carry):
            at = pl.multiple_of(c * 16, 16)
            rows = {s: basis[s, pl.ds(at, 16), :] for s in slots}
            return tuple(acc + fold(rows[a] * rows[b]) for acc, (_, a, b) in zip(carry, pairs))

        carry = tuple(jnp.zeros((8, 128), F32) for _ in pairs)
        carry = lax.fori_loop(0, chunks, body, carry, unroll=4)
        for (i, _, _), acc in zip(pairs, carry):
            dots[i] = acc

    stages = (
        (near, near_s, near_r, near_peer, near_me, GROUPS * LINE),
        (far, far_s, far_r, far_peer, sheet, SHEET),
    )

    def reduce_send(call, which, message):
        buffer, send, recv, peer, mine, n = stages[which]
        buffer[call, mine] = jnp.broadcast_to(message, (8, 128))
        own = buffer.at[call, mine]
        for o in range(1, n):
            remote(own, own, send.at[call, o], recv.at[call, mine], peer(o)[1]).start()

    def reduce_wait(call, which):
        buffer, send, recv, peer, mine, n = stages[which]
        own = buffer.at[call, mine]
        for o in range(1, n):
            other, who = peer(o)
            slot = buffer.at[call, other]
            remote(slot, slot, send.at[call, o], recv.at[call, other], who).wait_recv()
        for o in range(1, n):
            remote(own, own, send.at[call, o], recv.at[call, mine], peer(o)[1]).wait_send()
        total = buffer[call, 0]
        for i in range(1, n):
            total = total + buffer[call, i]
        return total

    def reduce_start(call, count):
        total = jnp.sum(dots[...], axis=1)
        column = jnp.sum(total, axis=1, keepdims=True)
        lane = lax.broadcasted_iota(jnp.int32, (24, 128), 1)
        place = lax.broadcasted_iota(jnp.int32, (24, 128), 0)
        keep = (lane == place) & (place < count)
        reduce_send(call, 0, jnp.sum(jnp.where(keep, column, 0.0), axis=0, keepdims=True))

    def reduce_middle(call):
        reduce_send(call, 1, reduce_wait(call, 0))

    def reduce_end(call, count):
        total = reduce_wait(call, 1)
        return [jnp.broadcast_to(total[:, i : i + 1], (8, 128)) for i in range(count)]

    def peer_copies(snap):
        block = table.at[snap, pl.ds(pl.multiple_of(me * 8, 8), 8)]
        return [remote(block, block, peer_s.at[snap], peer_r.at[snap], core_peer(grp, dom, o)) for o in range(1, DOMS)]

    def wait_peers(snap):
        arrived = table.at[snap, pl.ds(0, 8 * (DOMS - 1))]
        copy = remote(arrived, arrived, peer_s.at[snap], peer_r.at[snap], core_peer(grp, dom, 1))
        copy.wait_recv()
        copy.wait_send()

    def core_block(snap, which):
        return table.at[snap, pl.ds(pl.multiple_of(which * 512, 512), 512)]

    def core_copy(snap):
        block = core_block(snap, grp)
        return remote(block, block, core_s.at[snap], core_r.at[snap], other_core)

    def wait_core(snap):
        block = core_block(snap, 1 - grp)
        remote(block, block, core_s.at[snap], core_r.at[snap], other_core).wait_recv()
        core_copy(snap).wait_send()

    def start_all(copies):
        for copy in copies:
            copy.start()

    def write_to(ref):
        def write(i, row):
            ref[i : i + 1, :] = row

        return write

    def first_copies():
        return [
            remote(ref.at[pl.ds(at, PLANE)], first.at[1 - side, i], first_s.at[side, i], first_r.at[1 - side, i], who)
            for side, at, _, who in sides
            for i, ref in enumerate((vel, mass))
        ]

    for copy in loads:
        copy.wait()
    for e in (0, 3, 1, 2):
        rows = pl.ds(e * 256, 256)
        store_inner(basis.at[0], vel, e, force[rows, :] - (1.0 / GAIN) * products(vel, e), -PENALTY)
    expand(0, True, (0, 3))
    pl.semaphore_wait(barrier, len(greeted))
    start_all(first_copies())
    exchange_send(0, 0)
    expand(0, True, (1, 2))
    onehot_rows(sample, hot_sample)
    keys[...] = jnp.where(valid[...] != 0, source[...] * NODES + target_node[...], NODES * NODES)
    for copy in first_copies():
        copy.wait()
    for side in range(2):
        outer(0, side, first[side, 0], -PENALTY)
    expand(0, True, (0, 3))
    for copy in exchange_copies(0):
        copy.wait()
    for side, at, _, _ in sides:
        own = basis[0, at : at + PLANE, :]
        given = PENALTY * vel[at : at + PLANE, :]
        mapped = edge_map(side, given)
        then = outer(1, side, ghost[0, side, 0] + given, 0.5 * pull)
        beside[side, 0] = ghost[0, side, 1] + 0.5 * mapped - (0.5 * pull) * own
        beside[side, 1] = (
            ghost[0, side, 2] + 0.5 * edge_map(side, mapped - pull * own) + (0.5 * REACH - 1.0) * given - pull * then
        )

    for step in range(STEPS):
        call = 2 * step
        if step > 0:
            expand(0, True, (0, 3))
            exchange_send(2 * step, 0)
            expand(0, True, (1, 2))
            picked = []
            pick(out[...], sample, hot_sample, lambda i, row: picked.append(row))
            table[step - 1, pl.ds(pl.multiple_of(me * 8, 8), 8), :] = jnp.concatenate(picked, axis=0)
            exchange_wait(2 * step, 0, True)
        follow(1)
        index = {}
        for j in range(4):
            for i in range(min(j, 2) + 1):
                index[i, j] = index[j, i] = len(index) - sum(1 for a, b in index if a > b)
        accumulate([(n, i, j) for (i, j), n in index.items() if i <= j], 64)
        reduce_start(call, 9)
        expand(3, False, (0, 3))
        exchange_send(2 * step + 1, 3)
        expand(3, False, (1, 2))
        reduce_middle(call)
        if step == 0:
            onehot_rows(part, hot_part)
        else:
            start_all(peer_copies(step - 1))
        exchange_wait(2 * step + 1, 3, False)
        follow(4)
        m = reduce_end(call, 9)
        gram = [[m[index[i, j]] for j in range(3)] for i in range(4)]
        image = image_rows(gram, 3)
        head = [[image[max(i, j)][min(i, j)] for j in range(3)] for i in range(3)]
        opening = solve(head, gram[0])
        after_three = [-c for c in image_coefs(opening)]
        after_three[0] = 1.0 + after_three[0]
        combos = [after_three, shifted(after_three)]
        for _ in range(2):
            combos.append([2.0 * c for c in shifted(combos[-1])])
            for i, c in enumerate(combos[-3]):
                combos[-1][i] = combos[-1][i] - c
        factors = [[wide(c) for c in coefs] for coefs in combos]
        pairs = [(i, 4 + j) for j in range(3) for i in range(4)]
        pairs += [(4 + i, 4 + j) for j in range(4) for i in range(min(j, 2) + 1)]

        def gather_dots(c, carry):
            at = pl.multiple_of(c * 16, 16)
            rows = [basis[s, pl.ds(at, 16), :] for s in range(7)]
            for coefs in factors:
                value = coefs[0] * rows[0]
                for c_i, row in zip(coefs[1:], rows[1:7]):
                    value = value + c_i * row
                rows.append(value)
            held = rows[:4] + rows[7:]
            return tuple(acc + fold(held[a] * held[b]) for acc, (a, b) in zip(carry, pairs))

        carry = lax.fori_loop(0, 64, gather_dots, tuple(jnp.zeros((8, 128), F32) for _ in pairs))
        for i, acc in enumerate(carry):
            dots[i] = acc
        reduce_start(call + 1, len(pairs))
        if step > 0:
            wait_peers(step - 1)
            core_copy(step - 1).start()
        reduce_middle(call + 1)
        if step > 0:
            wait_core(step - 1)
            pick(table[step - 1], part, hot_part, write_to(feats))
        m = reduce_end(call + 1, len(pairs))
        index = {}
        for n, (a, b) in enumerate(pairs):
            index[a, b] = index[b, a] = n
        cross = image_rows([[m[index[i, 4 + j]] for j in range(3)] for i in range(4)], 3)
        gram = [[m[index[4 + i, 4 + j]] for j in range(3)] for i in range(4)]
        image = image_rows(gram, 3)
        whole = [[None] * 6 for _ in range(6)]
        for i in range(3):
            for j in range(3):
                whole[i][j] = head[i][j]
                whole[3 + i][3 + j] = image[max(i, j)][min(i, j)]
                whole[i][3 + j] = whole[3 + j][i] = cross[i][j]
        coefs = solve(whole, [m[index[i, 4]] for i in range(3)] + gram[0])
        moves = merged([(None, opening), (None, coefs[:3])] + [(coefs[3 + j], combos[j]) for j in range(3)])
        lost = image_coefs(coefs[3:])
        rest = merged([(None, combos[0])] + [(-lost[j], combos[j]) for j in range(4)] + [(-1.0, image_coefs(coefs[:3]))])
        moves = [wide(c) for c in moves]
        rest = [wide(c) for c in rest]
        start = vel if step == 0 else out
        more = step < STEPS - 1

        def advance(c, carry):
            rows = pl.ds(pl.multiple_of(c * 16, 16), 16)
            held = [basis[s, rows, :] for s in range(7 if more else 6)]
            moved = moves[0] * held[0]
            for c_i, row in zip(moves[1:], held[1:]):
                moved = moved + c_i * row
            if more:
                value = mass[rows, :] * moved
                for c_i, row in zip(rest, held):
                    value = value + c_i * row
                basis[0, rows, :] = value
            out[rows, :] = start[rows, :] + moved
            return carry

        lax.fori_loop(0, 64, advance, 0, unroll=2)

    last = STEPS - 1
    store = pltpu.make_async_copy(out, out_hbm, local.at[2])
    store.start()
    picked = []
    pick(out[...], sample, hot_sample, lambda i, row: picked.append(row))
    table[last, pl.ds(pl.multiple_of(me * 8, 8), 8), :] = jnp.concatenate(picked, axis=0)
    start_all(peer_copies(last))
    wait_peers(last)
    core_copy(last).start()
    here, there = (pl.ds(pl.multiple_of(which * 512, 512), 512) for which in (grp, 1 - grp))
    pick(table[last, here, :], part, hot_part.at[here], write_to(target))
    wait_core(last)

    def add_to(i, row):
        target[i : i + 1, :] = target[i : i + 1, :] + row

    pick(table[last, there, :], part, hot_part.at[there], add_to)
    store.wait()


VMEM = pl.BlockSpec(memory_space=pltpu.VMEM)
SMEM = pl.BlockSpec(memory_space=pltpu.SMEM)
ANY = pl.BlockSpec(memory_space=pl.ANY)


def run_steps(velocity, forcing, mass, sample, part, source, target_node, valid):
    dma = pltpu.SemaphoreType.DMA
    return pl.pallas_call(
        steps_kernel,
        out_shape=(
            jax.ShapeDtypeStruct((ROWS, 256), F32),
            jax.ShapeDtypeStruct((8, 256), F32),
            jax.ShapeDtypeStruct((8, 256), F32),
            jax.ShapeDtypeStruct((64, 128), jnp.int32),
        ),
        in_specs=[VMEM, ANY, ANY] + [VMEM] * 8,
        out_specs=(ANY, VMEM, VMEM, VMEM),
        scratch_shapes=[
            pltpu.VMEM((ROWS, 256), F32),
            pltpu.VMEM((ROWS, 256), F32),
            pltpu.VMEM((ROWS, 256), F32),
            dma((3,)),
            pltpu.VMEM((7, ROWS, 256), F32),
            pltpu.VMEM((4, 2, 3, PLANE, 256), F32),
            pltpu.VMEM((4, 2, 3, PLANE, 256), F32),
            pltpu.VMEM((2, 2, PLANE, 256), F32),
            pltpu.VMEM((2, 2, PLANE, 256), F32),
            pltpu.VMEM((24, 8, 128), F32),
            pltpu.VMEM((4, 8, 8, 128), F32),
            pltpu.VMEM((4, 16, 8, 128), F32),
            pltpu.VMEM((2, ROWS, 256), F32),
            pltpu.VMEM((ROWS, NODES), BF16),
            pltpu.VMEM((ROWS, NODES), BF16),
            dma((4, 2)), dma((4, 2)),
            dma((2, 2)), dma((2, 2)),
            dma((4, 8)), dma((4, 8)),
            dma((4, 16)), dma((4, 16)),
            dma((2,)), dma((2,)),
            dma((2,)), dma((2,)),
        ],
        compiler_params=pltpu.CompilerParams(
            collective_id=0, has_side_effects=True, vmem_limit_bytes=56 << 20
        ),
        cost_estimate=pl.CostEstimate(flops=30_000_000_000, bytes_accessed=4 << 20, transcendentals=0),
        name="viscous_steps",
    )(velocity, forcing, mass, sample, part, source, target_node, valid, *field_matrices())


def split3(value, axis):
    high, low = split(value)
    return jnp.concatenate([high, high, low], axis=axis)


def split3_other(value, axis):
    high, low = split(value)
    return jnp.concatenate([high, low, high], axis=axis)


HALF_PAGES = 8
COUNT_ROWS = HALF_PAGES * NODES


def count_edges(key_ref, adj, accs):
    def clear(i, carry):
        for acc in accs:
            acc[pl.ds(pl.multiple_of(i * 128, 128), 128), :] = jnp.zeros((128, 128), jnp.int32)
        return carry

    lax.fori_loop(0, COUNT_ROWS // 128, clear, 0)
    place = lax.broadcasted_iota(jnp.int32, (8, 128), 0) * 128 + lax.broadcasted_iota(jnp.int32, (8, 128), 1)
    stream = EDGES // len(accs)

    def add(i, carry):
        for u in range(8):
            keys = [key_ref[c * stream + i * 8 + u] for c in range(len(accs))]
            spots = [pl.ds(pl.multiple_of((k >> 11) * 8, 8), 8) for k in keys]
            held = [acc[spot, :] for acc, spot in zip(accs, spots)]
            for acc, spot, k, value in zip(accs, spots, keys, held):
                word = jnp.full((8, 128), k, jnp.int32)
                one = lax.shift_left(jnp.full((8, 128), 1, jnp.int32), (word >> 6) & 16)
                acc[spot, :] = value + jnp.where((word & 1023) == place, one, 0)
        return carry

    lax.fori_loop(0, stream // 8, add, 0)

    def total(i, carry):
        rows = pl.ds(pl.multiple_of(i * 128, 128), 128)
        value = accs[0][rows, :]
        for acc in accs[1:]:
            value = value + acc[rows, :]
        accs[0][rows, :] = value
        return carry

    lax.fori_loop(0, COUNT_ROWS // 128, total, 0, unroll=2)

    def halves(rows):
        value = accs[0][rows, :]
        return (value & 65535).astype(F32), (value >> 16).astype(F32)

    worst = jnp.zeros((128, 128), F32)
    for page in range(HALF_PAGES):

        def move(i, most):
            at = pl.multiple_of(i * 128, 128)
            for h, value in enumerate(halves(page_rows(at, page, 128))):
                low = value.astype(BF16)
                column = h * 1024 + page * 128
                adj[pl.ds(at, 128), column : column + 128] = low
                most = jnp.maximum(most, jnp.abs(value - low.astype(F32)))
            return most

        worst = lax.fori_loop(0, NODES // 128, move, worst, unroll=2)
    flagged = jnp.max(worst) > 0.0

    @pl.when(flagged)
    def _():
        def keep(i, carry):
            rows = pl.ds(pl.multiple_of(i * 128, 128), 128)
            for acc, value in zip(accs, halves(rows)):
                acc[rows, :] = (value - value.astype(BF16).astype(F32)).astype(jnp.int32)
            return carry

        lax.fori_loop(0, COUNT_ROWS // 128, keep, 0)

    return flagged


def page_rows(start, page, count):
    return pl.ds(start * 8 + page, count, stride=8)


def surrogate_kernel(
    key_ref, feats, target, w_in_ref, b_in_ref, bias_ref, w_out_ref, weights, field,
    out, field_out,
    one, two, three, four, adj, feat_row, target_row, state_0, state_1, agg_0, agg_1, slope_0, slope_1, partial_0, partial_1,
    sent_0, sent_1, sent_2, sent_3, back_agg, extra, grads_0, grads_1, w_fwd, w_bwd, field_hold, sem,
):
    tiles = NODES // 256
    states, aggs, slopes, partials = (state_0, state_1), (agg_0, agg_1), (slope_0, slope_1), (partial_0, partial_1)
    sent, grads = (sent_0, sent_1, sent_2, sent_3), (grads_0, grads_1)
    field_in = pltpu.make_async_copy(field, field_hold, sem.at[0])
    field_in.start()
    accs = (one, two, three, four)
    flagged = count_edges(key_ref, adj, accs)
    field_in.wait()
    field_back = pltpu.make_async_copy(field_hold, field_out, sem.at[1])
    field_back.start()
    for i in range(8):
        feat_row[:, i * 256 : (i + 1) * 256] = feats[i : i + 1, :]
        target_row[:, i * 256 : (i + 1) * 256] = target[i : i + 1, :]
    vectors = [w_in_ref[...], b_in_ref[...], bias_ref[...], w_out_ref[...], jnp.zeros((123, 128), F32)]
    columns = jnp.concatenate(vectors, axis=0).T
    w_in, b_in, w_out = columns[:, 0:1], columns[:, 1:2], columns[:, 4:5]
    biases = (columns[:, 2:3], columns[:, 3:4])
    for layer in range(LAYERS):
        weight = weights[layer]
        w_fwd[layer] = split3_other(weight.T, 1)
        w_bwd[layer] = split3_other(weight, 1)
    for ref in grads:
        ref[...] = jnp.zeros_like(ref)
    extra[...] = jnp.zeros_like(extra)

    def lanes(j):
        return pl.ds(pl.multiple_of(j * 256, 256), 256)

    def send(slot, at, value):
        high, low = split(value)
        sent[slot][0:128, at] = high
        sent[slot][128:256, at] = low

    def both(rows):
        return rows[:128] + rows[128:]

    def spill(half, rows):
        return accs[half][rows, :].astype(F32).astype(BF16)

    def gather_extra(slot):
        @pl.when(flagged)
        def _():
            for half in range(2):

                def body(page, carry):
                    rows = both(mm(sent[slot][...], spill(half, page_rows(0, page, NODES))))
                    extra[:, pl.ds(pl.multiple_of(half * 1024 + page * 128, 128), 128)] = rows
                    return carry

                lax.fori_loop(0, HALF_PAGES, body, 0)

    def scatter_extra(slot):
        @pl.when(flagged)
        def _():
            def body(j, carry):
                rows = jnp.zeros((256, 256), F32)
                for half in range(2):
                    for page in range(HALF_PAGES):
                        column = half * 1024 + page * 128
                        block = spill(half, page_rows(j * 256, page, 256))
                        rows = rows + mm_lanes(sent[slot][:, column : column + 128], block)
                extra[:, lanes(j)] = both(rows)
                return carry

            lax.fori_loop(0, tiles, body, 0)

    def gather(slot, into):
        gather_extra(slot)

        def body(j, carry):
            at = lanes(j)
            into[:, at] = AGG_SCALE * (both(mm(sent[slot][...], adj[:, at])) + extra[:, at])
            return carry

        lax.fori_loop(0, tiles, body, 0, unroll=8)

    def scatter(slot):
        scatter_extra(slot)

        def body(j, carry):
            at = lanes(j)
            back_agg[:, at] = AGG_SCALE * (both(mm_lanes(sent[slot][...], adj[at, :])) + extra[:, at])
            return carry

        lax.fori_loop(0, tiles, body, 0, unroll=8)

    def opening(j, carry):
        at = lanes(j)
        value = jnp.tanh(w_in * feat_row[:, at] + b_in)
        states[0][:, at] = value
        send(0, at, value)
        return carry

    lax.fori_loop(0, tiles, opening, 0, unroll=2)

    def joined(layer, at):
        return jnp.concatenate([states[layer][:, at], aggs[layer][:, at]], axis=0)

    def update(layer, at):
        bump = jnp.tanh(mm(w_fwd[layer], split3(joined(layer, at), 0)) + biases[layer])
        slopes[layer][:, at] = 1.0 - bump * bump
        return states[layer][:, at] + bump

    def back(layer, at, above):
        pre = above * slopes[layer][:, at]
        grads[layer][...] = grads[layer][...] + mm_lanes(split3(joined(layer, at), 1), split3_other(pre, 1))
        below = mm(w_bwd[layer], split3(pre, 0))
        partials[layer][:, at] = above + below[:128]
        send(2 + layer, at, below[128:])
        return jnp.sum(pre, axis=1, keepdims=True)

    def second(j, carry):
        at = lanes(j)
        value = update(0, at)
        states[1][:, at] = value
        send(1, at, value)
        return carry

    gather(0, agg_0)
    lax.fori_loop(0, tiles, second, 0, unroll=8)

    zero = jnp.zeros((128, 1), F32)

    def third(j, carry):
        loss, grad_out, grad_bias = carry
        at = lanes(j)
        value = update(1, at)
        miss = jnp.sum(w_out * value, axis=0, keepdims=True) - target_row[:, at]
        scaled = miss * (2.0 / (NODES * GROUPS * DOMS))
        loss = loss + miss * miss
        grad_out = grad_out + jnp.sum(value * scaled, axis=1, keepdims=True)
        return loss, grad_out, grad_bias + back(1, at, w_out * scaled)

    gather(1, agg_1)
    loss, grad_out, bias_1 = lax.fori_loop(
        0, tiles, third, (jnp.zeros((1, 256), F32), zero, zero), unroll=8
    )

    def fourth(j, carry):
        at = lanes(j)
        return carry + back(0, at, partials[1][:, at] + back_agg[:, at])

    scatter(3)
    bias_0 = lax.fori_loop(0, tiles, fourth, zero, unroll=8)

    def fifth(j, carry):
        grad_in, grad_bias = carry
        at = lanes(j)
        value = states[0][:, at]
        pre = (partials[0][:, at] + back_agg[:, at]) * (1.0 - value * value)
        grad_in = grad_in + jnp.sum(pre * feat_row[:, at], axis=1, keepdims=True)
        return grad_in, grad_bias + jnp.sum(pre, axis=1, keepdims=True)

    scatter(2)
    grad_in, grad_bias = lax.fori_loop(0, tiles, fifth, (zero, zero), unroll=8)
    loss = jnp.sum(loss, axis=1, keepdims=True) * (1.0 / (NODES * GROUPS * DOMS))
    lane = lax.broadcasted_iota(jnp.int32, (128, 128), 1)
    packed = jnp.where(lane == 5, loss, 0.0)
    for i, column in enumerate((grad_in, grad_bias, bias_0, bias_1, grad_out)):
        packed = packed + jnp.where(lane == i, column, 0.0)
    blank = jnp.zeros((3, 128), F32)
    for f in range(128):
        out[f, 0:4, :] = grads[f // 64][f % 64 * 4 : f % 64 * 4 + 4, :]
        out[f, 4:5, :] = packed[f : f + 1, :]
        out[f, 5:8, :] = blank
    field_back.wait()


def surrogate(key, feats, target, w_in, b_in, layer_bias, w_out, layer_weights, field):
    return pl.pallas_call(
        surrogate_kernel,
        out_shape=(jax.ShapeDtypeStruct((128, 8, 128), F32), jax.ShapeDtypeStruct((ROWS, 256), F32)),
        in_specs=[SMEM] + [VMEM] * 7 + [ANY],
        out_specs=(VMEM, ANY),
        scratch_shapes=[pltpu.VMEM((COUNT_ROWS + 8, 128), jnp.int32)] * 4
        + [
            pltpu.VMEM((NODES, NODES), BF16),
            pltpu.VMEM((1, NODES), F32),
            pltpu.VMEM((1, NODES), F32),
        ]
        + [pltpu.VMEM((128, NODES), F32)] * 8
        + [pltpu.VMEM((256, NODES), BF16)] * 4
        + [pltpu.VMEM((128, NODES), F32)] * 2
        + [pltpu.VMEM((256, 128), F32)] * 2
        + [
            pltpu.VMEM((LAYERS, 128, 768), BF16),
            pltpu.VMEM((LAYERS, 256, 384), BF16),
            pltpu.VMEM((ROWS, 256), F32),
            pltpu.SemaphoreType.DMA((2,)),
        ],
        compiler_params=pltpu.CompilerParams(vmem_limit_bytes=62 << 20),
        name="surrogate",
    )(
        key, feats, target, w_in.reshape(1, 128), b_in.reshape(1, 128), layer_bias, w_out.reshape(1, 128),
        layer_weights, field,
    )


def sum_kernel(
    grads_hbm, out, grads, local, other, total, share, result, core_s, core_r, share_s, share_r, back_s, back_r, last_s, last_r
):
    grp = lax.axis_index("grp")
    dom = lax.axis_index("dom")
    other_core = (1 - grp, dom)
    peers = [core_peer(grp, dom, o) for o in range(1, DOMS)]

    def remote(src, dst, send, recv, who):
        return pltpu.make_async_remote_copy(
            src_ref=src, dst_ref=dst, send_sem=send, recv_sem=recv, device_id=who, device_id_type=MESH
        )

    load = pltpu.make_async_copy(grads_hbm, grads, local)
    load.start()
    barrier = pltpu.get_barrier_semaphore()
    for who in peers + [other_core]:
        pl.semaphore_signal(barrier, inc=1, device_id=who, device_id_type=MESH)
    load.wait()
    pl.semaphore_wait(barrier, DOMS)

    def half(which):
        return pl.ds(pl.multiple_of(which * DOMS, DOMS), DOMS)

    copy = remote(grads.at[half(1 - grp)], other, core_s, core_r, other_core)
    copy.start()
    copy.wait()
    total[...] = grads[half(grp)] + other[...]
    for _, peer in peers:
        remote(total.at[peer], share.at[dom], share_s, share_r, (grp, peer)).start()
    share[dom] = total[dom]
    arrived = share.at[pl.ds(0, DOMS - 1)]
    copy = remote(arrived, arrived, share_s, share_r, peers[0])
    copy.wait_recv()
    copy.wait_send()
    parts = [share[i] for i in range(DOMS)]
    while len(parts) > 1:
        parts = [a + b for a, b in zip(parts[::2], parts[1::2])]
    mine = grp * DOMS + dom
    result[mine] = parts[0]
    for who in peers:
        remote(result.at[mine], result.at[mine], back_s, back_r, who).start()
    arrived = result.at[pl.ds(0, DOMS - 1)]
    copy = remote(arrived, arrived, back_s, back_r, peers[0])
    copy.wait_recv()
    copy.wait_send()
    own = result.at[half(grp)]
    copy = remote(own, own, last_s, last_r, other_core)
    copy.start()
    out[half(grp)] = result[half(grp)]
    there = result.at[half(1 - grp)]
    remote(there, there, last_s, last_r, other_core).wait_recv()
    out[half(1 - grp)] = result[half(1 - grp)]
    copy.wait_send()


def sum_grads(grads):
    dma = pltpu.SemaphoreType.DMA
    return pl.pallas_call(
        sum_kernel,
        out_shape=jax.ShapeDtypeStruct((128, 8, 128), F32),
        in_specs=[ANY],
        out_specs=VMEM,
        scratch_shapes=[
            pltpu.VMEM((2 * DOMS, 8, 128), F32),
            dma,
            pltpu.VMEM((DOMS, 8, 128), F32),
            pltpu.VMEM((DOMS, 8, 128), F32),
            pltpu.VMEM((DOMS, 8, 128), F32),
            pltpu.VMEM((2 * DOMS, 8, 128), F32),
        ]
        + [dma] * 8,
        compiler_params=pltpu.CompilerParams(collective_id=1, has_side_effects=True, vmem_limit_bytes=60 << 20),
        name="sum_grads",
    )(grads)


def unpack_kernel(tiles, weight_out, in_out, bias_in_out, bias_out, head_out, loss_out):
    for f in range(128):
        weight_out[f // 64, f % 64 * 4 : f % 64 * 4 + 4, :] = tiles[f, 0:4, :]
    rows = tiles[:, 4, :].T
    in_out[...] = rows[0:1, :]
    bias_in_out[...] = rows[1:2, :]
    bias_out[...] = rows[2:4, :]
    head_out[...] = rows[4:5, :]
    loss_out[...] = rows[5:6, 0:1]


def unpack(tiles):
    row = jax.ShapeDtypeStruct((1, 128), F32)
    return pl.pallas_call(
        unpack_kernel,
        out_shape=(
            jax.ShapeDtypeStruct((LAYERS, 256, 128), F32), row, row, jax.ShapeDtypeStruct((2, 128), F32), row,
            jax.ShapeDtypeStruct((1, 1), F32),
        ),
        in_specs=[VMEM],
        out_specs=(VMEM,) * 6,
        compiler_params=pltpu.CompilerParams(vmem_limit_bytes=60 << 20),
        name="unpack",
    )(tiles)


def shards(
    velocity, forcing, mass, sample_index, partition, edge_source, edge_target, edge_valid,
    w_in, b_in, layer_weights, layer_bias, w_out,
):
    shape = velocity.shape
    field, feats, target, keys = run_steps(
        velocity.reshape(ROWS, 256), forcing.reshape(ROWS, 256), mass.reshape(ROWS, 256),
        sample_index.reshape(16, 128), partition.reshape(16, 128),
        edge_source.reshape(64, 128), edge_target.reshape(64, 128), edge_valid.reshape(64, 128),
    )
    grads, field = surrogate(
        keys.reshape(EDGES), feats, target, w_in, b_in, layer_bias, w_out, layer_weights, field,
    )
    weight, grad_in, grad_bin, bias, head, loss = unpack(sum_grads(grads))
    return (
        field.reshape(shape), loss.reshape(()), grad_in.reshape(128), grad_bin.reshape(128), weight, bias,
        head.reshape(128),
    )


def solution(mesh):
    many = P(("grp", "dom"))
    block = P(("grp", "dom"), None, None)
    return jax.shard_map(
        shards,
        mesh=mesh,
        in_specs=(block,) * 3 + (many,) * 5 + (P(),) * 5,
        out_specs=(block,) + (P(),) * 6,
        check_vma=False,
    )
```

```python
import functools

import jax
import jax.numpy as jnp
import ml_dtypes
import numpy as np
from jax import lax
from jax.experimental import pallas as pl
from jax.experimental.pallas import tpu as pltpu
from jax.sharding import PartitionSpec as P

MESH = pl.DeviceIdType.MESH
F32 = jnp.float32
BF16 = jnp.bfloat16

STEPS = 2
LAYERS = 2
PENALTY = 2.0
AGG_SCALE = 0.25
NODES = 2048
EDGES = 8192
ROWS = 1024
PLANE = 32
GROUPS, DOMS, LINE, SHEET = 2, 64, 4, 16

CENTER = 14.125
HALF = 12.575
GAIN = 2.0 / HALF
PIVOT = 1e-6
REACH = GAIN * GAIN * float(sum(np.exp(-2.0 * i) for i in range(1, 8)))
CHIP_ORDER = [0] + sorted(
    range(1, DOMS), key=lambda o: -sum(min(c, 4 - c) for c in (o % 4, o // 4 % 4, o // 16))
)
FAR_ORDER = [0] + sorted(range(1, 16), key=lambda o: -(min(o % 4, 4 - o % 4) + min(o // 4, 4 - o // 4)))


def split_np(matrix):
    high = matrix.astype(np.float32).astype(ml_dtypes.bfloat16)
    low = (matrix - high.astype(np.float64)).astype(np.float32).astype(ml_dtypes.bfloat16)
    return high, low


def element_matrix():
    at = np.arange(8)
    return 2.5 * np.eye(8) - np.exp(-np.abs(at[:, None] - at[None, :]).astype(np.float64))


def line_matrix(length, wrap):
    matrix = np.kron(np.eye(length // 8), element_matrix())
    for last in range(7, length, 8):
        follow = (last + 1) % length
        if follow == 0 and not wrap:
            continue
        matrix[last, last] += PENALTY
        matrix[follow, follow] += PENALTY
        matrix[last, follow] -= PENALTY
        matrix[follow, last] -= PENALTY
    return matrix


def field_matrices():
    ends = np.zeros(8)
    ends[0] = ends[7] = PENALTY
    sheet = np.kron(element_matrix() + np.diag(ends), np.eye(32)) + np.kron(np.eye(8), line_matrix(32, False))
    sheet_high, sheet_low = split_np(GAIN * sheet)
    span_high, span_low = split_np(GAIN * line_matrix(256, True))
    left = np.concatenate([sheet_high, sheet_low, sheet_high], axis=1)
    right = np.concatenate([span_high, span_low, span_high], axis=0)
    edge = np.concatenate([sheet_high[:32, :32], sheet_low[:32, :32], sheet_high[:32, :32]], axis=1)
    return left, right, edge


def split(value):
    high = value.astype(BF16)
    return high, (value - high.astype(F32)).astype(BF16)


def mm(left, right):
    return jnp.dot(left, right, preferred_element_type=F32)


def mm_lanes(left, right):
    return lax.dot_general(left, right, (((1,), (1,)), ((), ())), preferred_element_type=F32)


def wide(tile):
    two = jnp.concatenate([tile, tile], axis=1)
    return jnp.concatenate([two, two], axis=0)


def fold(value):
    half = value[:8] + value[8:]
    return half[:, :128] + half[:, 128:]


def solve(matrix, rhs):
    n = len(rhs)
    rows = [list(row) for row in matrix]
    right = list(rhs)
    lower = {}
    inverse = []
    for k in range(n):
        pivot = rows[k][k]
        inverse.append(jnp.where(pivot > PIVOT * matrix[k][k], 1.0 / pivot, 0.0))
        for i in range(k + 1, n):
            factor = rows[k][i] * inverse[k]
            lower[i, k] = factor
            for j in range(i, n):
                rows[i][j] = rows[i][j] - factor * rows[k][j]
            right[i] = right[i] - factor * right[k]
    out = [None] * n
    for k in reversed(range(n)):
        value = right[k] * inverse[k]
        for i in range(k + 1, n):
            value = value - lower[i, k] * out[i]
        out[k] = value
    return out


def image_rows(gram, count):
    out = []
    for i in range(count):
        out.append(
            [CENTER * a + (0.5 * HALF) * (b + c) for a, b, c in zip(gram[i], gram[i + 1], gram[abs(i - 1)])]
        )
    return out


def image_coefs(coefs):
    out = [None] * (len(coefs) + 1)

    def add(at, value):
        out[at] = value if out[at] is None else out[at] + value

    for j, c in enumerate(coefs):
        add(j, CENTER * c)
        if j == 0:
            add(1, HALF * c)
        else:
            add(j + 1, (0.5 * HALF) * c)
            add(j - 1, (0.5 * HALF) * c)
    return out


def index_row(index_ref, i):
    return jnp.concatenate([index_ref[2 * i : 2 * i + 1, :], index_ref[2 * i + 1 : 2 * i + 2, :]], axis=1)


def onehot_rows(index_ref, out_ref):
    for i in range(8):
        row = index_row(index_ref, i) >> 8

        def body(c, carry):
            at = pl.multiple_of(c * 128, 128)
            place = lax.broadcasted_iota(jnp.int32, (128, 256), 0) + at
            out_ref[pl.ds(at, 128), i * 256 : (i + 1) * 256] = jnp.where(place == row, 1.0, 0.0).astype(BF16)
            return carry

        lax.fori_loop(0, ROWS // 128, body, 0)


def pick(table, index_ref, onehot_ref, write):
    both = jnp.concatenate(split(table.T), axis=0)
    place = lax.broadcasted_iota(jnp.int32, (256, 256), 0)
    for i in range(8):
        rows = mm(both, onehot_ref[:, i * 256 : (i + 1) * 256])
        rows = rows[:256] + rows[256:]
        column = index_row(index_ref, i) & 255
        write(i, jnp.sum(jnp.where(place == column, rows, 0.0), axis=0, keepdims=True))


def shifted(coefs):
    out = [None] * (len(coefs) + 1)

    def add(at, value):
        out[at] = value if out[at] is None else out[at] + value

    for i, c in enumerate(coefs):
        if i == 0:
            add(1, c)
        else:
            add(i + 1, 0.5 * c)
            add(i - 1, 0.5 * c)
    return out


def merged(parts):
    out = []
    for factor, coefs in parts:
        for i, c in enumerate(coefs):
            value = c if factor is None else factor * c
            if i < len(out):
                out[i] = out[i] + value
            else:
                out.append(value)
    return out


def core_peer(grp, dom, o):
    hop = CHIP_ORDER[o]
    y, z, x = (dom // 16 + hop // 16) % 4, (dom // 4 + hop // 4) % 4, (dom + hop) % 4
    return grp, y * 16 + z * 4 + x


def steps_kernel(
    vel, force_hbm, mass_hbm, sample, part, source, target_node, valid, left_mat, right_mat, edge_mat,
    out_hbm, feats, target, keys,
    force, mass, out, local, basis, stage, ghost, first, beside, dots, near, far, table, hot_sample, hot_part,
    halo_s, halo_r, first_s, first_r, near_s, near_r, far_s, far_r, peer_s, peer_r, core_s, core_r,
):
    grp = lax.axis_index("grp")
    dom = lax.axis_index("dom")
    me = grp * DOMS + dom
    line = dom % LINE
    sheet = dom // LINE
    near_me = grp * LINE + line

    def near_peer(o):
        other = (near_me + o) % (GROUPS * LINE)
        return other, (other // LINE, sheet * LINE + other % LINE)

    def far_peer(o):
        hop = FAR_ORDER[o]
        other = (sheet // 4 + hop // 4) % 4 * 4 + (sheet + hop) % 4
        return other, (grp, other * LINE + line)

    other_core = (1 - grp, dom)
    after = (me + 1) % (GROUPS * DOMS)
    before = (me + GROUPS * DOMS - 1) % (GROUPS * DOMS)
    after_id = (after // DOMS, after % DOMS)
    before_id = (before // DOMS, before % DOMS)

    loads = [
        pltpu.make_async_copy(force_hbm, force, local.at[0]),
        pltpu.make_async_copy(mass_hbm, mass, local.at[1]),
    ]
    for copy in loads:
        copy.start()
    barrier = pltpu.get_barrier_semaphore()
    greeted = [core_peer(grp, dom, o) for o in range(1, DOMS)] + [near_peer(o)[1] for o in range(1, 8)]
    greeted += [after_id, before_id]
    for who in greeted:
        pl.semaphore_signal(barrier, inc=1, device_id=who, device_id_type=MESH)

    def remote(src, dst, send, recv, who):
        return pltpu.make_async_remote_copy(
            src_ref=src, dst_ref=dst, send_sem=send, recv_sem=recv, device_id=who, device_id_type=MESH
        )

    sides = ((0, 0, 0, before_id), (1, ROWS - PLANE, 7, after_id))
    pull = PENALTY * GAIN

    def products(source, e):
        high, low = split(source[e * 256 : (e + 1) * 256, :])
        rows = mm(left_mat[...], jnp.concatenate([high, high, low], axis=0))
        return rows + mm(jnp.concatenate([high, high, low], axis=1), right_mat[...])

    def store_inner(dest, source, e, value, scale):
        at = e * 256
        top, bottom = value[:PLANE], value[256 - PLANE :]
        if e > 0:
            top = top - scale * source[at - PLANE : at, :]
        if e < 3:
            bottom = bottom - scale * source[at + 256 : at + 256 + PLANE, :]
        dest[at : at + PLANE, :] = top
        dest[at + PLANE : at + 256 - PLANE, :] = value[PLANE : 256 - PLANE]
        dest[at + 256 - PLANE : at + 256, :] = bottom

    def expand(slot, opening, elements):
        src, dst = basis.at[slot], basis.at[slot + 1]
        for e in elements:
            rows = pl.ds(e * 256, 256)
            value = products(src, e) + (GAIN * mass[rows, :] - GAIN * CENTER) * src[rows, :]
            if opening:
                value = 0.5 * value
            else:
                value = value - basis[slot - 1, rows, :]
            store_inner(dst, src, e, value, pull * (0.5 if opening else 1.0))

    def outer(slot, side, plane, scale):
        at = sides[side][1]
        value = basis[slot, at : at + PLANE, :] - scale * plane
        basis[slot, at : at + PLANE, :] = value
        return value

    def along(plane, level, near_rows):
        high, low = split(plane)
        wide_plane = jnp.concatenate([high, high, low], axis=1)
        return near_rows + mm(wide_plane, right_mat[...]) + (GAIN * level - GAIN * CENTER) * plane

    def edge_map(side, plane):
        high, low = split(plane)
        rows = mm(edge_mat[...], jnp.concatenate([high, high, low], axis=0))
        return along(plane, first[side, 1], rows)

    def exchange_copies(ex):
        return [
            remote(stage.at[ex, side], ghost.at[ex, 1 - side], halo_s.at[ex, side], halo_r.at[ex, 1 - side], who)
            for side, _, _, who in sides
        ]

    def exchange_send(ex, slot):
        for side, at, place, _ in sides:
            e = 0 if side == 0 else 3
            high, low = split(basis[slot + 1, e * 256 : (e + 1) * 256, :])
            rows = mm(left_mat[place * PLANE : (place + 1) * PLANE, :], jnp.concatenate([high, high, low], axis=0))
            plane = basis[slot + 1, at : at + PLANE, :]
            own = basis[slot, at : at + PLANE, :]
            stage[ex, side, 0] = own
            stage[ex, side, 1] = plane
            stage[ex, side, 2] = along(plane, mass[at : at + PLANE, :], rows) - own
        for copy in exchange_copies(ex):
            copy.start()

    def exchange_wait(ex, slot, opening):
        for copy in exchange_copies(ex):
            copy.wait()
        scale = pull * (0.5 if opening else 1.0)
        for side, at, _, _ in sides:
            own = basis[slot, at : at + PLANE, :]
            then = outer(slot + 1, side, ghost[ex, side, 0], scale)
            beside[side, 0] = ghost[ex, side, 1] - scale * own
            beside[side, 1] = ghost[ex, side, 2] - scale * edge_map(side, own) - pull * then

    def follow(slot):
        for k in range(2):
            expand(slot + k, False, range(4))
            for side in range(2):
                outer(slot + k + 1, side, beside[side, k], pull)

    def accumulate(pairs, chunks):
        slots = sorted({a for _, a, _ in pairs} | {b for _, _, b in pairs})

        def body(c, carry):
            at = pl.multiple_of(c * 16, 16)
            rows = {s: basis[s, pl.ds(at, 16), :] for s in slots}
            return tuple(acc + fold(rows[a] * rows[b]) for acc, (_, a, b) in zip(carry, pairs))

        carry = tuple(jnp.zeros((8, 128), F32) for _ in pairs)
        carry = lax.fori_loop(0, chunks, body, carry, unroll=4)
        for (i, _, _), acc in zip(pairs, carry):
            dots[i] = acc

    stages = (
        (near, near_s, near_r, near_peer, near_me, GROUPS * LINE),
        (far, far_s, far_r, far_peer, sheet, SHEET),
    )

    def reduce_send(call, which, message):
        buffer, send, recv, peer, mine, n = stages[which]
        buffer[call, mine] = jnp.broadcast_to(message, (8, 128))
        own = buffer.at[call, mine]
        for o in range(1, n):
            remote(own, own, send.at[call], recv.at[call], peer(o)[1]).start()

    def reduce_wait(call, which):
        buffer, send, recv, peer, mine, n = stages[which]
        arrived = buffer.at[call, pl.ds(0, n - 1)]
        copy = remote(arrived, arrived, send.at[call], recv.at[call], peer(1)[1])
        copy.wait_recv()
        copy.wait_send()
        parts = [buffer[call, i] for i in range(n)]
        while len(parts) > 1:
            parts = [a + b for a, b in zip(parts[::2], parts[1::2])]
        return parts[0]

    def reduce_start(call, count):
        total = jnp.sum(dots[...], axis=1)
        column = jnp.sum(total, axis=1, keepdims=True)
        lane = lax.broadcasted_iota(jnp.int32, (24, 128), 1)
        place = lax.broadcasted_iota(jnp.int32, (24, 128), 0)
        keep = (lane == place) & (place < count)
        reduce_send(call, 0, jnp.sum(jnp.where(keep, column, 0.0), axis=0, keepdims=True))

    def reduce_middle(call):
        reduce_send(call, 1, reduce_wait(call, 0))

    def reduce_end(call, count):
        total = reduce_wait(call, 1)
        return [jnp.broadcast_to(total[:, i : i + 1], (8, 128)) for i in range(count)]

    def peer_copies(snap):
        block = table.at[snap, pl.ds(pl.multiple_of(me * 8, 8), 8)]
        return [remote(block, block, peer_s.at[snap], peer_r.at[snap], core_peer(grp, dom, o)) for o in range(1, DOMS)]

    def wait_peers(snap):
        arrived = table.at[snap, pl.ds(0, 8 * (DOMS - 1))]
        copy = remote(arrived, arrived, peer_s.at[snap], peer_r.at[snap], core_peer(grp, dom, 1))
        copy.wait_recv()
        copy.wait_send()

    def core_block(snap, which):
        return table.at[snap, pl.ds(pl.multiple_of(which * 512, 512), 512)]

    def core_copy(snap):
        block = core_block(snap, grp)
        return remote(block, block, core_s.at[snap], core_r.at[snap], other_core)

    def wait_core(snap):
        block = core_block(snap, 1 - grp)
        remote(block, block, core_s.at[snap], core_r.at[snap], other_core).wait_recv()
        core_copy(snap).wait_send()

    def start_all(copies):
        for copy in copies:
            copy.start()

    def write_to(ref):
        def write(i, row):
            ref[i : i + 1, :] = row

        return write

    def first_copies():
        return [
            remote(ref.at[pl.ds(at, PLANE)], first.at[1 - side, i], first_s.at[side, i], first_r.at[1 - side, i], who)
            for side, at, _, who in sides
            for i, ref in enumerate((vel, mass))
        ]

    for copy in loads:
        copy.wait()
    for e in (0, 3, 1, 2):
        rows = pl.ds(e * 256, 256)
        store_inner(basis.at[0], vel, e, force[rows, :] - (1.0 / GAIN) * products(vel, e), -PENALTY)
    expand(0, True, (0, 3))
    pl.semaphore_wait(barrier, len(greeted))
    start_all(first_copies())
    exchange_send(0, 0)
    expand(0, True, (1, 2))
    onehot_rows(sample, hot_sample)
    keys[...] = jnp.where(valid[...] != 0, source[...] * NODES + target_node[...], NODES * NODES)
    for copy in first_copies():
        copy.wait()
    for side in range(2):
        outer(0, side, first[side, 0], -PENALTY)
    expand(0, True, (0, 3))
    for copy in exchange_copies(0):
        copy.wait()
    for side, at, _, _ in sides:
        own = basis[0, at : at + PLANE, :]
        given = PENALTY * vel[at : at + PLANE, :]
        mapped = edge_map(side, given)
        then = outer(1, side, ghost[0, side, 0] + given, 0.5 * pull)
        beside[side, 0] = ghost[0, side, 1] + 0.5 * mapped - (0.5 * pull) * own
        beside[side, 1] = (
            ghost[0, side, 2] + 0.5 * edge_map(side, mapped - pull * own) + (0.5 * REACH - 1.0) * given - pull * then
        )

    for step in range(STEPS):
        call = 2 * step
        if step > 0:
            expand(0, True, (0, 3))
            exchange_send(2 * step, 0)
            expand(0, True, (1, 2))
            picked = []
            pick(out[...], sample, hot_sample, lambda i, row: picked.append(row))
            table[step - 1, pl.ds(pl.multiple_of(me * 8, 8), 8), :] = jnp.concatenate(picked, axis=0)
            start_all(peer_copies(step - 1))
            exchange_wait(2 * step, 0, True)
        follow(1)
        index = {}
        for j in range(4):
            for i in range(min(j, 2) + 1):
                index[i, j] = index[j, i] = len(index) - sum(1 for a, b in index if a > b)
        accumulate([(n, i, j) for (i, j), n in index.items() if i <= j], 64)
        reduce_start(call, 9)
        expand(3, False, (0, 3))
        exchange_send(2 * step + 1, 3)
        expand(3, False, (1, 2))
        reduce_middle(call)
        if step == 0:
            onehot_rows(part, hot_part)
        exchange_wait(2 * step + 1, 3, False)
        follow(4)
        m = reduce_end(call, 9)
        gram = [[m[index[i, j]] for j in range(3)] for i in range(4)]
        image = image_rows(gram, 3)
        head = [[image[max(i, j)][min(i, j)] for j in range(3)] for i in range(3)]
        opening = solve(head, gram[0])
        after_three = [-c for c in image_coefs(opening)]
        after_three[0] = 1.0 + after_three[0]
        combos = [after_three, shifted(after_three)]
        for _ in range(2):
            combos.append([2.0 * c for c in shifted(combos[-1])])
            for i, c in enumerate(combos[-3]):
                combos[-1][i] = combos[-1][i] - c
        factors = [[wide(c) for c in coefs] for coefs in combos]
        pairs = [(i, 4 + j) for j in range(3) for i in range(4)]
        pairs += [(4 + i, 4 + j) for j in range(4) for i in range(min(j, 2) + 1)]

        def gather_dots(c, carry):
            at = pl.multiple_of(c * 16, 16)
            rows = [basis[s, pl.ds(at, 16), :] for s in range(7)]
            for coefs in factors:
                value = coefs[0] * rows[0]
                for c_i, row in zip(coefs[1:], rows[1:7]):
                    value = value + c_i * row
                rows.append(value)
            held = rows[:4] + rows[7:]
            return tuple(acc + fold(held[a] * held[b]) for acc, (a, b) in zip(carry, pairs))

        carry = lax.fori_loop(0, 64, gather_dots, tuple(jnp.zeros((8, 128), F32) for _ in pairs))
        for i, acc in enumerate(carry):
            dots[i] = acc
        reduce_start(call + 1, len(pairs))
        if step > 0:
            wait_peers(step - 1)
            core_copy(step - 1).start()
        reduce_middle(call + 1)
        if step > 0:
            wait_core(step - 1)
            pick(table[step - 1], part, hot_part, write_to(feats))
        m = reduce_end(call + 1, len(pairs))
        index = {}
        for n, (a, b) in enumerate(pairs):
            index[a, b] = index[b, a] = n
        cross = image_rows([[m[index[i, 4 + j]] for j in range(3)] for i in range(4)], 3)
        gram = [[m[index[4 + i, 4 + j]] for j in range(3)] for i in range(4)]
        image = image_rows(gram, 3)
        whole = [[None] * 6 for _ in range(6)]
        for i in range(3):
            for j in range(3):
                whole[i][j] = head[i][j]
                whole[3 + i][3 + j] = image[max(i, j)][min(i, j)]
                whole[i][3 + j] = whole[3 + j][i] = cross[i][j]
        coefs = solve(whole, [m[index[i, 4]] for i in range(3)] + gram[0])
        moves = merged([(None, opening), (None, coefs[:3])] + [(coefs[3 + j], combos[j]) for j in range(3)])
        lost = image_coefs(coefs[3:])
        rest = merged([(None, combos[0])] + [(-lost[j], combos[j]) for j in range(4)] + [(-1.0, image_coefs(coefs[:3]))])
        moves = [wide(c) for c in moves]
        rest = [wide(c) for c in rest]
        start = vel if step == 0 else out
        more = step < STEPS - 1

        def advance(c, carry):
            rows = pl.ds(pl.multiple_of(c * 16, 16), 16)
            held = [basis[s, rows, :] for s in range(7 if more else 6)]
            moved = moves[0] * held[0]
            for c_i, row in zip(moves[1:], held[1:]):
                moved = moved + c_i * row
            if more:
                value = mass[rows, :] * moved
                for c_i, row in zip(rest, held):
                    value = value + c_i * row
                basis[0, rows, :] = value
            out[rows, :] = start[rows, :] + moved
            return carry

        lax.fori_loop(0, 64, advance, 0, unroll=2)

    last = STEPS - 1
    store = pltpu.make_async_copy(out, out_hbm, local.at[2])
    store.start()
    picked = []
    pick(out[...], sample, hot_sample, lambda i, row: picked.append(row))
    table[last, pl.ds(pl.multiple_of(me * 8, 8), 8), :] = jnp.concatenate(picked, axis=0)
    start_all(peer_copies(last))
    wait_peers(last)
    core_copy(last).start()
    here, there = (pl.ds(pl.multiple_of(which * 512, 512), 512) for which in (grp, 1 - grp))
    pick(table[last, here, :], part, hot_part.at[here], write_to(target))
    wait_core(last)

    def add_to(i, row):
        target[i : i + 1, :] = target[i : i + 1, :] + row

    pick(table[last, there, :], part, hot_part.at[there], add_to)
    store.wait()


VMEM = pl.BlockSpec(memory_space=pltpu.VMEM)
SMEM = pl.BlockSpec(memory_space=pltpu.SMEM)
ANY = pl.BlockSpec(memory_space=pl.ANY)


def run_steps(velocity, forcing, mass, sample, part, source, target_node, valid):
    dma = pltpu.SemaphoreType.DMA
    return pl.pallas_call(
        steps_kernel,
        out_shape=(
            jax.ShapeDtypeStruct((ROWS, 256), F32),
            jax.ShapeDtypeStruct((8, 256), F32),
            jax.ShapeDtypeStruct((8, 256), F32),
            jax.ShapeDtypeStruct((64, 128), jnp.int32),
        ),
        in_specs=[VMEM, ANY, ANY] + [VMEM] * 8,
        out_specs=(ANY, VMEM, VMEM, VMEM),
        scratch_shapes=[
            pltpu.VMEM((ROWS, 256), F32),
            pltpu.VMEM((ROWS, 256), F32),
            pltpu.VMEM((ROWS, 256), F32),
            dma((3,)),
            pltpu.VMEM((7, ROWS, 256), F32),
            pltpu.VMEM((4, 2, 3, PLANE, 256), F32),
            pltpu.VMEM((4, 2, 3, PLANE, 256), F32),
            pltpu.VMEM((2, 2, PLANE, 256), F32),
            pltpu.VMEM((2, 2, PLANE, 256), F32),
            pltpu.VMEM((24, 8, 128), F32),
            pltpu.VMEM((4, 8, 8, 128), F32),
            pltpu.VMEM((4, 16, 8, 128), F32),
            pltpu.VMEM((2, ROWS, 256), F32),
            pltpu.VMEM((ROWS, NODES), BF16),
            pltpu.VMEM((ROWS, NODES), BF16),
            dma((4, 2)), dma((4, 2)),
            dma((2, 2)), dma((2, 2)),
            dma((4,)), dma((4,)),
            dma((4,)), dma((4,)),
            dma((2,)), dma((2,)),
            dma((2,)), dma((2,)),
        ],
        compiler_params=pltpu.CompilerParams(
            collective_id=0, has_side_effects=True, vmem_limit_bytes=56 << 20
        ),
        cost_estimate=pl.CostEstimate(flops=30_000_000_000, bytes_accessed=4 << 20, transcendentals=0),
        name="viscous_steps",
    )(velocity, forcing, mass, sample, part, source, target_node, valid, *field_matrices())


def split3(value, axis):
    high, low = split(value)
    return jnp.concatenate([high, high, low], axis=axis)


def split3_other(value, axis):
    high, low = split(value)
    return jnp.concatenate([high, low, high], axis=axis)


HALF_PAGES = 8
COUNT_ROWS = HALF_PAGES * NODES


def count_edges(key_ref, adj, accs):
    def clear(i, carry):
        for acc in accs:
            acc[pl.ds(pl.multiple_of(i * 128, 128), 128), :] = jnp.zeros((128, 128), jnp.int32)
        return carry

    lax.fori_loop(0, COUNT_ROWS // 128, clear, 0)
    place = lax.broadcasted_iota(jnp.int32, (8, 128), 0) * 128 + lax.broadcasted_iota(jnp.int32, (8, 128), 1)
    stream = EDGES // len(accs)

    def add(i, carry):
        for u in range(8):
            keys = [key_ref[c * stream + i * 8 + u] for c in range(len(accs))]
            spots = [pl.ds(pl.multiple_of((k >> 11) * 8, 8), 8) for k in keys]
            held = [acc[spot, :] for acc, spot in zip(accs, spots)]
            for acc, spot, k, value in zip(accs, spots, keys, held):
                word = jnp.full((8, 128), k, jnp.int32)
                one = lax.shift_left(jnp.full((8, 128), 1, jnp.int32), (word >> 6) & 16)
                acc[spot, :] = value + jnp.where((word & 1023) == place, one, 0)
        return carry

    lax.fori_loop(0, stream // 8, add, 0)

    def total(i, carry):
        rows = pl.ds(pl.multiple_of(i * 128, 128), 128)
        value = accs[0][rows, :]
        for acc in accs[1:]:
            value = value + acc[rows, :]
        accs[0][rows, :] = value
        return carry

    lax.fori_loop(0, COUNT_ROWS // 128, total, 0, unroll=2)

    def halves(rows):
        value = accs[0][rows, :]
        return (value & 65535).astype(F32), (value >> 16).astype(F32)

    worst = jnp.zeros((128, 128), F32)
    for page in range(HALF_PAGES):

        def move(i, most):
            at = pl.multiple_of(i * 128, 128)
            for h, value in enumerate(halves(page_rows(at, page, 128))):
                low = value.astype(BF16)
                column = h * 1024 + page * 128
                adj[pl.ds(at, 128), column : column + 128] = low
                most = jnp.maximum(most, jnp.abs(value - low.astype(F32)))
            return most

        worst = lax.fori_loop(0, NODES // 128, move, worst, unroll=2)
    flagged = jnp.max(worst) > 0.0

    @pl.when(flagged)
    def _():
        def keep(i, carry):
            rows = pl.ds(pl.multiple_of(i * 128, 128), 128)
            for acc, value in zip(accs, halves(rows)):
                acc[rows, :] = (value - value.astype(BF16).astype(F32)).astype(jnp.int32)
            return carry

        lax.fori_loop(0, COUNT_ROWS // 128, keep, 0)

    return flagged


def page_rows(start, page, count):
    return pl.ds(start * 8 + page, count, stride=8)


def surrogate_kernel(
    key_ref, feats, target, w_in_ref, b_in_ref, bias_ref, w_out_ref, weights, field,
    out, field_out,
    one, two, three, four, adj, feat_row, target_row, state_0, state_1, agg_0, agg_1, slope_0, slope_1, partial_0, partial_1,
    sent_0, sent_1, sent_2, sent_3, back_agg, extra, grads_0, grads_1, w_fwd, w_bwd, field_hold, sem,
):
    tiles = NODES // 256
    states, aggs, slopes, partials = (state_0, state_1), (agg_0, agg_1), (slope_0, slope_1), (partial_0, partial_1)
    sent, grads = (sent_0, sent_1, sent_2, sent_3), (grads_0, grads_1)
    field_in = pltpu.make_async_copy(field, field_hold, sem.at[0])
    field_in.start()
    accs = (one, two, three, four)
    flagged = count_edges(key_ref, adj, accs)
    field_in.wait()
    field_back = pltpu.make_async_copy(field_hold, field_out, sem.at[1])
    field_back.start()
    for i in range(8):
        feat_row[:, i * 256 : (i + 1) * 256] = feats[i : i + 1, :]
        target_row[:, i * 256 : (i + 1) * 256] = target[i : i + 1, :]
    vectors = [w_in_ref[...], b_in_ref[...], bias_ref[...], w_out_ref[...], jnp.zeros((123, 128), F32)]
    columns = jnp.concatenate(vectors, axis=0).T
    w_in, b_in, w_out = columns[:, 0:1], columns[:, 1:2], columns[:, 4:5]
    biases = (columns[:, 2:3], columns[:, 3:4])
    for layer in range(LAYERS):
        weight = weights[layer]
        w_fwd[layer] = split3_other(weight.T, 1)
        w_bwd[layer] = split3_other(weight, 1)
    for ref in grads:
        ref[...] = jnp.zeros_like(ref)
    extra[...] = jnp.zeros_like(extra)

    def lanes(j):
        return pl.ds(pl.multiple_of(j * 256, 256), 256)

    def send(slot, at, value):
        high, low = split(value)
        sent[slot][0:128, at] = high
        sent[slot][128:256, at] = low

    def both(rows):
        return rows[:128] + rows[128:]

    def spill(half, rows):
        return accs[half][rows, :].astype(F32).astype(BF16)

    def gather_extra(slot):
        @pl.when(flagged)
        def _():
            for half in range(2):

                def body(page, carry):
                    rows = both(mm(sent[slot][...], spill(half, page_rows(0, page, NODES))))
                    extra[:, pl.ds(pl.multiple_of(half * 1024 + page * 128, 128), 128)] = rows
                    return carry

                lax.fori_loop(0, HALF_PAGES, body, 0)

    def scatter_extra(slot):
        @pl.when(flagged)
        def _():
            def body(j, carry):
                rows = jnp.zeros((256, 256), F32)
                for half in range(2):
                    for page in range(HALF_PAGES):
                        column = half * 1024 + page * 128
                        block = spill(half, page_rows(j * 256, page, 256))
                        rows = rows + mm_lanes(sent[slot][:, column : column + 128], block)
                extra[:, lanes(j)] = both(rows)
                return carry

            lax.fori_loop(0, tiles, body, 0)

    def gather(slot, into):
        gather_extra(slot)

        def body(j, carry):
            at = lanes(j)
            into[:, at] = AGG_SCALE * (both(mm(sent[slot][...], adj[:, at])) + extra[:, at])
            return carry

        lax.fori_loop(0, tiles, body, 0, unroll=8)

    def scatter(slot):
        scatter_extra(slot)

        def body(j, carry):
            at = lanes(j)
            back_agg[:, at] = AGG_SCALE * (both(mm_lanes(sent[slot][...], adj[at, :])) + extra[:, at])
            return carry

        lax.fori_loop(0, tiles, body, 0, unroll=8)

    def opening(j, carry):
        at = lanes(j)
        value = jnp.tanh(w_in * feat_row[:, at] + b_in)
        states[0][:, at] = value
        send(0, at, value)
        return carry

    lax.fori_loop(0, tiles, opening, 0, unroll=2)

    def joined(layer, at):
        return jnp.concatenate([states[layer][:, at], aggs[layer][:, at]], axis=0)

    def update(layer, at):
        bump = jnp.tanh(mm(w_fwd[layer], split3(joined(layer, at), 0)) + biases[layer])
        slopes[layer][:, at] = 1.0 - bump * bump
        return states[layer][:, at] + bump

    def back(layer, at, above):
        pre = above * slopes[layer][:, at]
        grads[layer][...] = grads[layer][...] + mm_lanes(split3(joined(layer, at), 1), split3_other(pre, 1))
        below = mm(w_bwd[layer], split3(pre, 0))
        partials[layer][:, at] = above + below[:128]
        send(2 + layer, at, below[128:])
        return jnp.sum(pre, axis=1, keepdims=True)

    def second(j, carry):
        at = lanes(j)
        value = update(0, at)
        states[1][:, at] = value
        send(1, at, value)
        return carry

    gather(0, agg_0)
    lax.fori_loop(0, tiles, second, 0, unroll=8)

    zero = jnp.zeros((128, 1), F32)

    def third(j, carry):
        loss, grad_out, grad_bias = carry
        at = lanes(j)
        value = update(1, at)
        miss = jnp.sum(w_out * value, axis=0, keepdims=True) - target_row[:, at]
        scaled = miss * (2.0 / (NODES * GROUPS * DOMS))
        loss = loss + miss * miss
        grad_out = grad_out + jnp.sum(value * scaled, axis=1, keepdims=True)
        return loss, grad_out, grad_bias + back(1, at, w_out * scaled)

    gather(1, agg_1)
    loss, grad_out, bias_1 = lax.fori_loop(
        0, tiles, third, (jnp.zeros((1, 256), F32), zero, zero), unroll=8
    )

    def fourth(j, carry):
        at = lanes(j)
        return carry + back(0, at, partials[1][:, at] + back_agg[:, at])

    scatter(3)
    bias_0 = lax.fori_loop(0, tiles, fourth, zero, unroll=8)

    def fifth(j, carry):
        grad_in, grad_bias = carry
        at = lanes(j)
        value = states[0][:, at]
        pre = (partials[0][:, at] + back_agg[:, at]) * (1.0 - value * value)
        grad_in = grad_in + jnp.sum(pre * feat_row[:, at], axis=1, keepdims=True)
        return grad_in, grad_bias + jnp.sum(pre, axis=1, keepdims=True)

    scatter(2)
    grad_in, grad_bias = lax.fori_loop(0, tiles, fifth, (zero, zero), unroll=8)
    loss = jnp.sum(loss, axis=1, keepdims=True) * (1.0 / (NODES * GROUPS * DOMS))
    lane = lax.broadcasted_iota(jnp.int32, (128, 128), 1)
    packed = jnp.where(lane == 5, loss, 0.0)
    for i, column in enumerate((grad_in, grad_bias, bias_0, bias_1, grad_out)):
        packed = packed + jnp.where(lane == i, column, 0.0)
    blank = jnp.zeros((3, 128), F32)
    for f in range(128):
        out[f, 0:4, :] = grads[f // 64][f % 64 * 4 : f % 64 * 4 + 4, :]
        out[f, 4:5, :] = packed[f : f + 1, :]
        out[f, 5:8, :] = blank
    field_back.wait()


def surrogate(key, feats, target, w_in, b_in, layer_bias, w_out, layer_weights, field):
    return pl.pallas_call(
        surrogate_kernel,
        out_shape=(jax.ShapeDtypeStruct((128, 8, 128), F32), jax.ShapeDtypeStruct((ROWS, 256), F32)),
        in_specs=[SMEM] + [VMEM] * 7 + [ANY],
        out_specs=(VMEM, ANY),
        scratch_shapes=[pltpu.VMEM((COUNT_ROWS + 8, 128), jnp.int32)] * 4
        + [
            pltpu.VMEM((NODES, NODES), BF16),
            pltpu.VMEM((1, NODES), F32),
            pltpu.VMEM((1, NODES), F32),
        ]
        + [pltpu.VMEM((128, NODES), F32)] * 8
        + [pltpu.VMEM((256, NODES), BF16)] * 4
        + [pltpu.VMEM((128, NODES), F32)] * 2
        + [pltpu.VMEM((256, 128), F32)] * 2
        + [
            pltpu.VMEM((LAYERS, 128, 768), BF16),
            pltpu.VMEM((LAYERS, 256, 384), BF16),
            pltpu.VMEM((ROWS, 256), F32),
            pltpu.SemaphoreType.DMA((2,)),
        ],
        compiler_params=pltpu.CompilerParams(vmem_limit_bytes=62 << 20),
        name="surrogate",
    )(
        key, feats, target, w_in.reshape(1, 128), b_in.reshape(1, 128), layer_bias, w_out.reshape(1, 128),
        layer_weights, field,
    )


def sum_kernel(
    grads_hbm, out, grads, local, other, total, share, result, core_s, core_r, share_s, share_r, back_s, back_r, last_s, last_r
):
    grp = lax.axis_index("grp")
    dom = lax.axis_index("dom")
    other_core = (1 - grp, dom)
    peers = [core_peer(grp, dom, o) for o in range(1, DOMS)]

    def remote(src, dst, send, recv, who):
        return pltpu.make_async_remote_copy(
            src_ref=src, dst_ref=dst, send_sem=send, recv_sem=recv, device_id=who, device_id_type=MESH
        )

    load = pltpu.make_async_copy(grads_hbm, grads, local)
    load.start()
    barrier = pltpu.get_barrier_semaphore()
    for who in peers + [other_core]:
        pl.semaphore_signal(barrier, inc=1, device_id=who, device_id_type=MESH)
    load.wait()
    pl.semaphore_wait(barrier, DOMS)

    def half(which):
        return pl.ds(pl.multiple_of(which * DOMS, DOMS), DOMS)

    copy = remote(grads.at[half(1 - grp)], other, core_s, core_r, other_core)
    copy.start()
    copy.wait()
    total[...] = grads[half(grp)] + other[...]
    for _, peer in peers:
        remote(total.at[peer], share.at[dom], share_s, share_r, (grp, peer)).start()
    share[dom] = total[dom]
    arrived = share.at[pl.ds(0, DOMS - 1)]
    copy = remote(arrived, arrived, share_s, share_r, peers[0])
    copy.wait_recv()
    copy.wait_send()
    parts = [share[i] for i in range(DOMS)]
    while len(parts) > 1:
        parts = [a + b for a, b in zip(parts[::2], parts[1::2])]
    mine = grp * DOMS + dom
    result[mine] = parts[0]
    for who in peers:
        remote(result.at[mine], result.at[mine], back_s, back_r, who).start()
    arrived = result.at[pl.ds(0, DOMS - 1)]
    copy = remote(arrived, arrived, back_s, back_r, peers[0])
    copy.wait_recv()
    copy.wait_send()
    own = result.at[half(grp)]
    copy = remote(own, own, last_s, last_r, other_core)
    copy.start()
    out[half(grp)] = result[half(grp)]
    there = result.at[half(1 - grp)]
    remote(there, there, last_s, last_r, other_core).wait_recv()
    out[half(1 - grp)] = result[half(1 - grp)]
    copy.wait_send()


def sum_grads(grads):
    dma = pltpu.SemaphoreType.DMA
    return pl.pallas_call(
        sum_kernel,
        out_shape=jax.ShapeDtypeStruct((128, 8, 128), F32),
        in_specs=[ANY],
        out_specs=VMEM,
        scratch_shapes=[
            pltpu.VMEM((2 * DOMS, 8, 128), F32),
            dma,
            pltpu.VMEM((DOMS, 8, 128), F32),
            pltpu.VMEM((DOMS, 8, 128), F32),
            pltpu.VMEM((DOMS, 8, 128), F32),
            pltpu.VMEM((2 * DOMS, 8, 128), F32),
        ]
        + [dma] * 8,
        compiler_params=pltpu.CompilerParams(collective_id=1, has_side_effects=True, vmem_limit_bytes=60 << 20),
        name="sum_grads",
    )(grads)


def unpack_kernel(tiles, weight_out, in_out, bias_in_out, bias_out, head_out, loss_out):
    for f in range(128):
        weight_out[f // 64, f % 64 * 4 : f % 64 * 4 + 4, :] = tiles[f, 0:4, :]
    rows = tiles[:, 4, :].T
    in_out[...] = rows[0:1, :]
    bias_in_out[...] = rows[1:2, :]
    bias_out[...] = rows[2:4, :]
    head_out[...] = rows[4:5, :]
    loss_out[...] = rows[5:6, 0:1]


def unpack(tiles):
    row = jax.ShapeDtypeStruct((1, 128), F32)
    return pl.pallas_call(
        unpack_kernel,
        out_shape=(
            jax.ShapeDtypeStruct((LAYERS, 256, 128), F32), row, row, jax.ShapeDtypeStruct((2, 128), F32), row,
            jax.ShapeDtypeStruct((1, 1), F32),
        ),
        in_specs=[VMEM],
        out_specs=(VMEM,) * 6,
        compiler_params=pltpu.CompilerParams(vmem_limit_bytes=60 << 20),
        name="unpack",
    )(tiles)


def shards(
    velocity, forcing, mass, sample_index, partition, edge_source, edge_target, edge_valid,
    w_in, b_in, layer_weights, layer_bias, w_out,
):
    shape = velocity.shape
    field, feats, target, keys = run_steps(
        velocity.reshape(ROWS, 256), forcing.reshape(ROWS, 256), mass.reshape(ROWS, 256),
        sample_index.reshape(16, 128), partition.reshape(16, 128),
        edge_source.reshape(64, 128), edge_target.reshape(64, 128), edge_valid.reshape(64, 128),
    )
    grads, field = surrogate(
        keys.reshape(EDGES), feats, target, w_in, b_in, layer_bias, w_out, layer_weights, field,
    )
    weight, grad_in, grad_bin, bias, head, loss = unpack(sum_grads(grads))
    return (
        field.reshape(shape), loss.reshape(()), grad_in.reshape(128), grad_bin.reshape(128), weight, bias,
        head.reshape(128),
    )


def solution(mesh):
    many = P(("grp", "dom"))
    block = P(("grp", "dom"), None, None)
    return jax.shard_map(
        shards,
        mesh=mesh,
        in_specs=(block,) * 3 + (many,) * 5 + (P(),) * 5,
        out_specs=(block,) + (P(),) * 6,
        check_vma=False,
    )
```
